256 devices in a mesh: sp: 32 (over x, z_lo, core), dp: 8 (over y, z_hi).
Axes of the slice: x: 4, y: 4, z: 8 (z_hi: 2, z_lo: 4; z = z_hi * 4 + z_lo), core: 2. Of those that a mesh axis runs over, the one named last changes fastest.
Arguments:
- queries: bfloat16 [8, 4096, 8192], P('dp', 'sp'), may hold values from -12.5 to 12.5
- key_before_rotary: bfloat16 [8, 4096, 1024], P('dp', 'sp'), may hold values from -5 to 5
- value_inputs: bfloat16 [8, 4096, 1024], P('dp', 'sp'), may hold values from -6 to 6
- out_grad: bfloat16 [8, 4096, 8192], P('dp', 'sp'), may hold values from -6 to 6
- layer_input: bfloat16 [8, 4096, 4096], P('dp', 'sp'), may hold values from -6 to 6
- group_first: int32 [8, 32], P('dp'), may hold values from 0 to 24, as said below
- seq_length: int32 [8, 32], P('dp'), may hold values from 512 to 2048, as said below
- pos_offset: int32 [8, 32], P('dp'), may hold values from 0 to 4095, as said below
Outputs:
- query_grad: bfloat16 [8, 4096, 8192], P('dp', 'sp')
- key_gradient: bfloat16 [8, 4096, 1024], P('dp', 'sp')
- value_gradient: bfloat16 [8, 4096, 1024], P('dp', 'sp')
- kproj_grad: float32 [4096, 1024], P(('sp', 'dp'))
The draws below stay inside these ranges and needn't reach their ends.
Inputs may be any that keep to these rules, and one draw needn't show every extreme that they name: `group_first`: each half of a row's devices holds either one group of 16 neighbouring devices or two aligned groups of 8; every device of a group holds the same first device, length and offset; in every draw the first group of row 0 has 16 devices. `seq_length`: A group of g devices holds a sequence of at least g * 64 and at most g * 128 tokens; the group starting at device 0 of row 0 is full. `pos_offset`: the group starting at device 0 of row 0 has offset 4095.
All inputs are finite; a program needn't handle non-finite values.
Results may differ from the reference program's by a relative error of at most 0.019.
Values may be sent and summed in bfloat16 or wider, within the bound.
No kernel may reach another device: no remote copies, remote signals or barrier semaphores. Data moves between devices by JAX's collectives and lax.ppermute only.
A program may use at most 128 MiB of HBM per device.

```python
import math
import jax
import jax.numpy as jnp
from jax import lax

QUERY_HEADS = 64
KEY_VALUE_HEADS = 8
HEAD_SIZE = 128
DW = 4096
TOK = 128
ROW_TOKEN_COUNT = 4096
N_SP = 32
N_DP = 8


def plan_tables(key):
    quarter = N_SP // 4
    split = jax.random.randint(jax.random.fold_in(key, 101), (N_DP, 2), 0, 2)
    split = split.at[0, 0].set(0)
    device = jnp.arange(N_SP, dtype=jnp.int32)[None, :]
    split_dev = jnp.repeat(split, N_SP // 2, axis=1)
    first = jnp.where(split_dev == 1, device // quarter * quarter, device // (2 * quarter) * (2 * quarter)).astype(jnp.int32)
    width = jnp.where(split_dev == 1, quarter, 2 * quarter).astype(jnp.int32)
    shorten = jax.random.randint(jax.random.fold_in(key, 102), (N_DP, N_SP), 0, N_SP // 8 * TOK + 1) * (width // quarter)
    shorten = jnp.take_along_axis(shorten, first, axis=1)
    row_zero = jnp.arange(N_DP, dtype=jnp.int32)[:, None] == 0
    shorten = jnp.where(row_zero & (first == 0), 0, shorten)
    length = (width * TOK - shorten).astype(jnp.int32)
    offset = jax.random.randint(jax.random.fold_in(key, 103), (N_DP, N_SP), 0, 4096)
    offset = offset.at[0, 0].set(4095)
    offset = jnp.take_along_axis(offset, first, axis=1).astype(jnp.int32)
    return (first, length, offset)


def draw_group_first(key, part):
    tables = plan_tables(key)
    return tables[0]


def draw_seq_length(key, part):
    tables = plan_tables(key)
    return tables[1]


def draw_pos_offset(key, part):
    tables = plan_tables(key)
    return tables[2]


def selected(key):
    chosen = jax.random.randint(jax.random.fold_in(key, 201), (N_DP, ROW_TOKEN_COUNT), 0, 48) == 0
    return chosen


def key_region(key, large_negative):
    chosen = selected(key)
    rotary_base = jnp.clip(jax.random.normal(jax.random.fold_in(key, 203), (N_DP, ROW_TOKEN_COUNT, KEY_VALUE_HEADS * HEAD_SIZE)), -3.0, 3.0)
    verbose_flag = jax.random.uniform(jax.random.fold_in(key, 204), (N_DP, ROW_TOKEN_COUNT, KEY_VALUE_HEADS * HEAD_SIZE), minval=-1.0, maxval=1.0) * large_negative
    return jnp.where(chosen[:, :, None] & (large_negative > 0.0), verbose_flag, rotary_base)


def draw_key_before_rotary(key, part):
    return key_region(key, 0.0).astype(jnp.bfloat16)


def draw_queries(key, part):
    own_key = jax.random.fold_in(key, 5)
    return jnp.clip(jax.random.normal(jax.random.fold_in(own_key, 2), (N_DP, ROW_TOKEN_COUNT, QUERY_HEADS * HEAD_SIZE)), -4.0, 4.0).astype(jnp.bfloat16)


def with_spikes(drawn, rng, source, target, blocks, factor):
    owner, partner = [(jnp.arange(drawn.shape[position]) // (drawn.shape[position] // blocks)).reshape([-1 if axis == position else 1 for axis in range(drawn.ndim)]) for position in (source, target)]
    chosen = jax.random.permutation(rng, blocks)[partner]
    strong = (owner == chosen) | (owner == (partner + blocks // 2) % blocks)
    return jnp.where(strong, factor * drawn, drawn)


def block_scale(rng, dims, shards, low, largest):
    level = 1.0
    for axis_at, parts in shards:
        heights = jax.random.uniform(jax.random.fold_in(jax.random.fold_in(rng, 6), axis_at), (parts,), jnp.float32, low / len(shards), largest / len(shards))
        level = level * jnp.repeat(jnp.exp(heights), dims[axis_at] // parts).reshape((-1,) + (1,) * (len(dims) - 1 - axis_at))
    return level


def bell_draw(key, dims, scale, limit, cuts=(), kind=jnp.bfloat16):
    entries = jax.random.normal(key, dims, jnp.float32) * scale
    if len(cuts) > 0:
        entries = block_scale(key, dims, cuts, -0.22, 0.18) * entries
    return jnp.clip(entries, min=-limit, max=limit).astype(kind)


def heavy_noise(key, dims, scale, reach, pieces, heavy, kind=jnp.bfloat16):
    drawn = scale * jax.random.normal(key, dims, jnp.float32)
    if pieces:
        drawn = drawn * block_scale(key, dims, pieces, -0.22, 0.18)
    return jnp.clip(with_spikes(drawn, jax.random.fold_in(key, 3), *heavy), -reach, reach).astype(kind)


def setup_inputs(seed: int = 0) -> dict:
    key_list = jax.random.split(jax.random.key(seed), 9)
    queries = draw_queries(jax.random.fold_in(key_list[8], 71), 0)
    key_before_rotary = draw_key_before_rotary(jax.random.fold_in(key_list[8], 71), 0)
    value_inputs = bell_draw(key_list[2], (N_DP, ROW_TOKEN_COUNT, KEY_VALUE_HEADS * HEAD_SIZE), 1.0, 6.0, ((0, 8), (1, 32)))
    out_grad = bell_draw(key_list[3], (N_DP, ROW_TOKEN_COUNT, QUERY_HEADS * HEAD_SIZE), 1.0, 6.0, ((0, 8), (1, 32)))
    layer_input = heavy_noise(key_list[4], (N_DP, ROW_TOKEN_COUNT, DW), 1.0, 6.0, ((0, 8), (1, 32)), (1, 2, 32, 2.75))
    group_first = draw_group_first(jax.random.fold_in(key_list[8], 71), 0)
    seq_length = draw_seq_length(jax.random.fold_in(key_list[8], 71), 0)
    pos_offset = draw_pos_offset(jax.random.fold_in(key_list[8], 71), 0)
    return dict(queries=queries, key_before_rotary=key_before_rotary, value_inputs=value_inputs, out_grad=out_grad, layer_input=layer_input, group_first=group_first, seq_length=seq_length, pos_offset=pos_offset)


def angles(positions):
    half_dim = HEAD_SIZE // 2
    rates = jnp.exp(jnp.arange(half_dim, dtype=jnp.float32) * (-2.0 * math.log(10000.0) / HEAD_SIZE))
    phase = positions.astype(jnp.float32)[:, None] * rates[None, :]
    return jnp.cos(phase)[:, None, :], jnp.sin(phase)[:, None, :]


def apply_rotary(field, cosine_table, sine_line):
    half_dim = field.shape[-1] // 2
    first_half = field[..., :half_dim]
    second_half = field[..., half_dim:]
    return jnp.concatenate([first_half * cosine_table - second_half * sine_line, second_half * cosine_table + first_half * sine_line], -1)


def inverse_rotary(field, cosine_table, sine_line):
    half_dim = field.shape[-1] // 2
    first_half = field[..., :half_dim]
    second_half = field[..., half_dim:]
    return jnp.concatenate([first_half * cosine_table + second_half * sine_line, second_half * cosine_table - first_half * sine_line], -1)


def attend(query_block, grad_block, key_block, value_block, query_index, key_index, query_seq, key_seq, key_valid):
    single = jnp.float32
    scaling = HEAD_SIZE ** -0.5
    scores = jnp.einsum('igrd,jgd->grij', query_block.astype(single), key_block.astype(single)) * scaling
    allowed = (query_seq[:, None] == key_seq[None, :]) & (key_index[None, :] <= query_index[:, None]) & key_valid[None, :]
    scores = jnp.where(allowed[None, None], scores, -1e30)
    row_peak = jnp.max(scores, axis=-1, keepdims=True)
    weights = jnp.exp(scores - row_peak)
    weights = weights / jnp.sum(weights, axis=-1, keepdims=True)
    rounded = weights.astype(jnp.bfloat16)
    prob_grad = jnp.einsum('igrd,jgd->grij', grad_block.astype(single), value_block.astype(single))
    value_part = jnp.einsum('grij,igrd->jgd', rounded.astype(single), grad_block.astype(single))
    row_dot = jnp.sum(weights * prob_grad, axis=-1, keepdims=True)
    score_grad = (weights * (prob_grad - row_dot) * scaling).astype(jnp.bfloat16)
    query_part = jnp.einsum('grij,jgd->igrd', score_grad.astype(single), key_block.astype(single))
    key_part = jnp.einsum('grij,igrd->jgd', score_grad.astype(single), query_block.astype(single))
    return query_part, key_part, value_part


def add_rows(accum, part, start_row):
    current = lax.dynamic_slice_in_dim(accum, start_row, part.shape[0], 0)
    return lax.dynamic_update_slice_in_dim(accum, current + part, start_row, 0)


def row_grads(inputs):
    query_row, key_line, value_line, gradient_line, first_row, length_row, offset_row = inputs
    tokens_per_row = query_row.shape[0]
    device_local_tokens = tokens_per_row // first_row.shape[0]
    device_of = jnp.arange(tokens_per_row, dtype=jnp.int32) // device_local_tokens
    inner_pos = jnp.arange(tokens_per_row, dtype=jnp.int32) % device_local_tokens
    seq_ids = jnp.repeat(first_row, device_local_tokens)
    local_pos = (device_of - seq_ids) * device_local_tokens + inner_pos
    row_valid_mask = local_pos < jnp.repeat(length_row, device_local_tokens)
    cosine_table, sine_line = angles(jnp.repeat(offset_row, device_local_tokens) + local_pos)
    group_width = QUERY_HEADS // KEY_VALUE_HEADS
    rotated_queries = apply_rotary(query_row.reshape(tokens_per_row, QUERY_HEADS, HEAD_SIZE).astype(jnp.float32), cosine_table, sine_line)
    rotated_queries = rotated_queries.astype(jnp.bfloat16).reshape(tokens_per_row, KEY_VALUE_HEADS, group_width, HEAD_SIZE)
    rotated_keys = apply_rotary(key_line.reshape(tokens_per_row, KEY_VALUE_HEADS, HEAD_SIZE).astype(jnp.float32), cosine_table, sine_line).astype(jnp.bfloat16)
    value_heads = value_line.reshape(tokens_per_row, KEY_VALUE_HEADS, HEAD_SIZE)
    incoming_gradient = jnp.where(row_valid_mask[:, None], gradient_line, jnp.zeros_like(gradient_line)).reshape(tokens_per_row, KEY_VALUE_HEADS, group_width, HEAD_SIZE)
    block_rows = 4 * device_local_tokens
    block_count = tokens_per_row // block_rows
    halved_rows = tokens_per_row // 2
    per_half = halved_rows // block_rows
    positions = jnp.arange(tokens_per_row, dtype=jnp.int32)

    def block_step(carry, block_id):
        key_running_sum, value_running_sum = carry
        start_row = block_id * block_rows
        half_start = (block_id // per_half) * halved_rows
        inner_block = block_id % per_half
        query_block = lax.dynamic_slice_in_dim(rotated_queries, start_row, block_rows, 0)
        grad_block = lax.dynamic_slice_in_dim(incoming_gradient, start_row, block_rows, 0)
        query_index = lax.dynamic_slice_in_dim(positions, start_row, block_rows, 0)
        query_seq = lax.dynamic_slice_in_dim(seq_ids, start_row, block_rows, 0)

        def make_branch(count):
            key_length = count * block_rows

            def branch(operand):
                def keyed(array):
                    return lax.dynamic_slice_in_dim(array, half_start, key_length, 0)
                query_part, key_part, value_part = attend(
                    query_block, grad_block, keyed(rotated_keys), keyed(value_heads), query_index, keyed(positions),
                    query_seq, keyed(seq_ids), keyed(row_valid_mask))
                padding_amount = jnp.zeros((halved_rows - key_length, KEY_VALUE_HEADS, HEAD_SIZE), jnp.float32)
                return query_part, jnp.concatenate([key_part, padding_amount], 0), jnp.concatenate([value_part, padding_amount], 0)
            return branch

        branches = [make_branch(count) for count in range(1, per_half + 1)]
        query_part, key_part, value_part = lax.switch(inner_block, branches, 0)
        key_running_sum = add_rows(key_running_sum, key_part, half_start)
        value_running_sum = add_rows(value_running_sum, value_part, half_start)
        return (key_running_sum, value_running_sum), query_part

    zero_filled = jnp.zeros((tokens_per_row, KEY_VALUE_HEADS, HEAD_SIZE), jnp.float32)
    (key_running_sum, value_running_sum), query_acc = lax.scan(block_step, (zero_filled, zero_filled), jnp.arange(block_count, dtype=jnp.int32))
    query_acc = query_acc.reshape(tokens_per_row, QUERY_HEADS, HEAD_SIZE)
    query_grad = inverse_rotary(query_acc, cosine_table, sine_line).astype(jnp.bfloat16).reshape(tokens_per_row, QUERY_HEADS * HEAD_SIZE)
    key_gradient = inverse_rotary(key_running_sum, cosine_table, sine_line).astype(jnp.bfloat16).reshape(tokens_per_row, KEY_VALUE_HEADS * HEAD_SIZE)
    value_gradient = value_running_sum.astype(jnp.bfloat16).reshape(tokens_per_row, KEY_VALUE_HEADS * HEAD_SIZE)
    return query_grad, key_gradient, value_gradient


def reference(queries, key_before_rotary, value_inputs, out_grad, layer_input, group_first, seq_length, pos_offset):
    query_grad, key_gradient, value_gradient = lax.map(row_grads, (queries, key_before_rotary, value_inputs, out_grad, group_first, seq_length, pos_offset))

    def add_batch_row(total_grad, operands):
        return total_grad + jnp.dot(operands[0].T, operands[1], preferred_element_type=jnp.float32), None

    start_grad = jnp.zeros((layer_input.shape[2], key_gradient.shape[2]), jnp.float32)
    kproj_grad, _unused = lax.scan(add_batch_row, start_grad, (layer_input, key_gradient))
    return query_grad, key_gradient, value_gradient, kproj_grad
```

```python
import math

import jax
import jax.numpy as jnp
from jax import lax
from jax.experimental import pallas as pl
from jax.experimental.pallas import tpu as pltpu
from jax.sharding import PartitionSpec as P

HEADS = 64
KV_HEADS = 8
D = 128
HALF = D // 2
TOK = 128
SP = 32
PARTS = 2
REP = HEADS // KV_HEADS
CHUNK = 2 * TOK
CHUNKS = 8
STACK = 2
ROWS = STACK * CHUNK
SCALE = D ** (-0.5)
LOG2E = 1.4426950408889634
MIB = 1 << 20

HALF_GROUPS = [list(range(16)), list(range(16, 32))]
QUAD_GROUPS = [
    [h * 16 + xl * 8 + z * 2 + c for xl in range(2) for c in range(2)]
    for h in range(2)
    for z in range(4)
]
Y_GROUPS = [
    [(x * 8 + z * 2 + c) * 8 + y * 2 + zh for c in range(2) for y in range(4)]
    for x in range(4)
    for z in range(4)
    for zh in range(2)
]
PLANE_GROUPS = [
    [s * 8 + y * 2 + zh for s in range(SP) for zh in range(2)] for y in range(4)
]


def swap(array, axes, groups):
    return lax.all_to_all(
        array, axes, split_axis=0, concat_axis=0, axis_index_groups=groups, tiled=True
    )


def params(limit=48):
    return pltpu.CompilerParams(vmem_limit_bytes=limit * MIB)


def cost(flops, nbytes):
    return pl.CostEstimate(flops=flops, bytes_accessed=nbytes, transcendentals=0)


def dot(a, b, dims):
    return lax.dot_general(a, b, (dims, ((), ())), preferred_element_type=jnp.float32)


def turn(x, cos, sin):
    return x * cos + pltpu.roll(x, HALF, 1) * sin


def key_prep_kernel(k_ref, v_ref, cos_ref, sin_ref, *outs):
    cos, sin = cos_ref[...], sin_ref[...]
    for part in range(PARTS):
        cols = slice(part * D, (part + 1) * D)
        k = turn(k_ref[:, cols].astype(jnp.float32), cos, sin).astype(jnp.bfloat16)
        v = v_ref[:, cols]
        for z in range(4):
            outs[part][0, z, 0, 0] = k
            outs[part][0, z, 0, 1] = v


def key_prep(k, v, cos, sin):
    table = pl.BlockSpec((TOK, D), lambda j: (0, 0))
    column = pl.BlockSpec((TOK, PARTS * D), lambda j: (0, j))
    shape = jax.ShapeDtypeStruct((2, 4, 2, 2, TOK, D), jnp.bfloat16)
    return pl.pallas_call(
        key_prep_kernel,
        grid=(4,),
        in_specs=[column, column, table, table],
        out_specs=[
            pl.BlockSpec((1, 4, 1, 2, TOK, D), lambda j: (j // 2, 0, j % 2, 0, 0, 0))
        ]
        * PARTS,
        out_shape=[shape] * PARTS,
        compiler_params=params(),
        cost_estimate=cost(1 << 20, 3 * MIB),
        name="key_prep",
    )(k, v, cos, sin)


def query_prep_kernel(q_ref, g_ref, cos_ref, sin_ref, valid_ref, *outs):
    cos, sin = cos_ref[...], sin_ref[...]
    keep = valid_ref[...] > 0.0
    for part in range(PARTS):
        for h in range(REP):
            cols = slice((part * REP + h) * D, (part * REP + h + 1) * D)
            q = turn(q_ref[:, cols].astype(jnp.float32), cos, sin)
            outs[part][0, 0, :, h * D : (h + 1) * D] = q.astype(jnp.bfloat16)
            g = jnp.where(keep, g_ref[:, cols].astype(jnp.float32), 0.0)
            outs[part][0, 1, :, h * D : (h + 1) * D] = g.astype(jnp.bfloat16)


def query_prep(q, g, cos, sin, valid):
    table = pl.BlockSpec((TOK, D), lambda j: (0, 0))
    column = pl.BlockSpec((TOK, PARTS * REP * D), lambda j: (0, j))
    shape = jax.ShapeDtypeStruct((4, 2, TOK, REP * D), jnp.bfloat16)
    return pl.pallas_call(
        query_prep_kernel,
        grid=(4,),
        in_specs=[column, column, table, table, table],
        out_specs=[pl.BlockSpec((1, 2, TOK, REP * D), lambda j: (j, 0, 0, 0))] * PARTS,
        out_shape=[shape] * PARTS,
        compiler_params=params(),
        cost_estimate=cost(8 << 20, 8 * MIB),
        name="query_prep",
    )(q, g, cos, sin, valid)


def input_prep_kernel(x_ref, out_ref):
    for s in range(4):
        xt = x_ref[:, s * TOK : (s + 1) * TOK].T
        for y in range(4):
            piece = xt[y * 32 : (y + 1) * 32]
            out_ref[0, y, s] = piece
            out_ref[1, y, s] = piece


def input_prep(x):
    return pl.pallas_call(
        input_prep_kernel,
        grid=(8,),
        in_specs=[pl.BlockSpec((TOK, 512), lambda i: (0, i))],
        out_specs=pl.BlockSpec((2, 4, 4, 32, TOK), lambda i: (0, 0, i, 0, 0)),
        out_shape=jax.ShapeDtypeStruct((2, 4, SP, 32, TOK), jnp.bfloat16),
        compiler_params=params(),
        cost_estimate=cost(1 << 20, 3 * MIB),
        name="input_prep",
    )(x)


def attention_kernel(
    meta_ref,
    qg_ref,
    kv_ref,
    cos_ref,
    sin_ref,
    dq_ref,
    dkv_ref,
    kt_ref,
    s_ref,
    dp_ref,
    dk_ref,
    dv_ref,
    dqt_ref,
):
    block, heads = pl.program_id(0), pl.program_id(1)
    low, diagonal, count = meta_ref[block, 0], meta_ref[block, 1], meta_ref[block, 2]

    def keys(p, which):
        return kv_ref[pl.ds(2 * p, 2), which].reshape(CHUNK, D)

    @pl.when((block == 0) & (heads == 0))
    def _():
        dk_ref[...] = jnp.zeros_like(dk_ref)
        dv_ref[...] = jnp.zeros_like(dv_ref)
        for p in range(CHUNKS):
            kt_ref[p] = keys(p, 0).T

    def stacked(which):
        return jnp.concatenate(
            [
                qg_ref[0, :, which, :, h * D : (h + 1) * D].reshape(CHUNK, D)
                for h in range(STACK)
            ],
            axis=0,
        )

    @pl.when(count <= 0)
    def _():
        dq_ref[...] = jnp.zeros_like(dq_ref)

    @pl.when(count > 0)
    def _():
        q, g = stacked(0), stacked(1)
        nt = ((1,), (1,))
        nn = ((1,), (0,))

        def score(p, peak):
            s = dot(keys(p, 0), q, nt)
            s_ref[p] = s
            dp_ref[p] = dot(keys(p, 1), g, nt)
            return jnp.maximum(peak, jnp.max(s, axis=0, keepdims=True))

        peak = lax.fori_loop(low, diagonal, score, jnp.full((1, ROWS), -1e30, jnp.float32))
        key_at = lax.broadcasted_iota(jnp.int32, (CHUNK, ROWS), 0)
        row_at = lax.broadcasted_iota(jnp.int32, (CHUNK, ROWS), 1) & (CHUNK - 1)
        allowed = (key_at <= row_at) & (key_at < count)
        s = jnp.where(allowed, dot(keys(diagonal, 0), q, nt), -1e30)
        s_ref[diagonal] = s
        dp_ref[diagonal] = dot(keys(diagonal, 1), g, nt)
        peak = jnp.maximum(peak, jnp.max(s, axis=0, keepdims=True))

        def weigh(p, sums):
            total, mixed = sums
            e = jnp.exp2((s_ref[p] - peak) * (SCALE * LOG2E))
            s_ref[p] = e
            return (
                total + jnp.sum(e, axis=0, keepdims=True),
                mixed + jnp.sum(e * dp_ref[p], axis=0, keepdims=True),
            )

        zero = jnp.zeros((1, ROWS), jnp.float32)
        total, mixed = lax.fori_loop(low, diagonal + 1, weigh, (zero, zero))
        inverse = 1.0 / total
        row_dot = mixed * inverse
        dqt_ref[...] = jnp.zeros_like(dqt_ref)

        def spread(p, carry):
            weights = s_ref[p] * inverse
            ds = (weights * (dp_ref[p] - row_dot)).astype(jnp.bfloat16)
            dv_ref[p] += dot(weights.astype(jnp.bfloat16), g, nn)
            dk_ref[p] += dot(ds, q, nn)
            dqt_ref[...] += dot(kt_ref[p], ds, nn)
            return carry

        lax.fori_loop(low, diagonal + 1, spread, 0)
        cos, sin = cos_ref[0], sin_ref[0]
        for h in range(STACK):
            cols = slice(h * CHUNK, (h + 1) * CHUNK)
            x1 = dqt_ref[:HALF, cols] * SCALE
            x2 = dqt_ref[HALF:, cols] * SCALE
            y = jnp.concatenate([x1 * cos + x2 * sin, x2 * cos - x1 * sin], axis=0)
            dq_ref[0, :, :, h * D : (h + 1) * D] = y.T.astype(jnp.bfloat16).reshape(2, TOK, D)

    @pl.when((block == 1) & (heads == REP // STACK - 1))
    def _():
        for p in range(CHUNKS):
            dk = (dk_ref[p] * SCALE).astype(jnp.bfloat16)
            dkv_ref[2 * p : 2 * p + 2, 0] = dk.reshape(2, TOK, D)
            dkv_ref[2 * p : 2 * p + 2, 1] = dv_ref[p].astype(jnp.bfloat16).reshape(2, TOK, D)


def attention(meta, qg, kv, cos, sin):
    width = STACK * D
    table = pl.BlockSpec((1, HALF, CHUNK), lambda b, h: (b, 0, 0))
    whole = pl.BlockSpec((16, 2, TOK, D), lambda b, h: (0, 0, 0, 0))
    return pl.pallas_call(
        attention_kernel,
        grid=(2, REP // STACK),
        in_specs=[
            pl.BlockSpec(memory_space=pltpu.SMEM),
            pl.BlockSpec((1, 2, 2, TOK, width), lambda b, h: (b, 0, 0, 0, h)),
            whole,
            table,
            table,
        ],
        out_specs=[
            pl.BlockSpec((1, 2, TOK, width), lambda b, h: (b, 0, 0, h)),
            whole,
        ],
        out_shape=[
            jax.ShapeDtypeStruct((2, 2, TOK, REP * D), jnp.bfloat16),
            jax.ShapeDtypeStruct((16, 2, TOK, D), jnp.bfloat16),
        ],
        scratch_shapes=[
            pltpu.VMEM((CHUNKS, D, CHUNK), jnp.bfloat16),
            pltpu.VMEM((CHUNKS, CHUNK, ROWS), jnp.float32),
            pltpu.VMEM((CHUNKS, CHUNK, ROWS), jnp.float32),
            pltpu.VMEM((CHUNKS, CHUNK, D), jnp.float32),
            pltpu.VMEM((CHUNKS, CHUNK, D), jnp.float32),
            pltpu.VMEM((D, ROWS), jnp.float32),
        ],
        compiler_params=params(),
        cost_estimate=cost(25 * 10**9, 6 * MIB),
        name="attention",
    )(meta, qg.reshape(2, 2, 2, TOK, REP * D), kv, cos, sin)


def key_post_kernel(a_ref, b_ref, cos_ref, sin_ref, dk_ref, dv_ref, kg_ref):
    cos, sin = cos_ref[...], sin_ref[...]
    for part, ref in enumerate((a_ref, b_ref)):
        cols = slice(part * D, (part + 1) * D)
        dk = ref[0, 0, 0, 0].astype(jnp.float32)
        dv = ref[0, 0, 0, 1].astype(jnp.float32)
        for z in range(1, 4):
            dk += ref[0, z, 0, 0].astype(jnp.float32)
            dv += ref[0, z, 0, 1].astype(jnp.float32)
        dk = turn(dk, cos, -sin).astype(jnp.bfloat16)
        dk_ref[:, cols] = dk
        dv_ref[:, cols] = dv.astype(jnp.bfloat16)
        for y in range(4):
            kg_ref[0, y, :, cols] = dk


def key_post(a, b, cos, sin):
    shape = (2, 4, 2, 2, TOK, D)
    table = pl.BlockSpec((TOK, D), lambda j: (0, 0))
    column = pl.BlockSpec((TOK, PARTS * D), lambda j: (0, j))
    source = pl.BlockSpec((1, 4, 1, 2, TOK, D), lambda j: (j // 2, 0, j % 2, 0, 0, 0))
    full = jax.ShapeDtypeStruct((TOK, KV_HEADS * D), jnp.bfloat16)
    return pl.pallas_call(
        key_post_kernel,
        grid=(4,),
        in_specs=[source, source, table, table],
        out_specs=[
            column,
            column,
            pl.BlockSpec((1, 4, TOK, PARTS * D), lambda j: (j // 2, 0, 0, j % 2)),
        ],
        out_shape=[full, full, jax.ShapeDtypeStruct((2, 4, TOK, 512), jnp.bfloat16)],
        compiler_params=params(),
        cost_estimate=cost(2 << 20, 4 * MIB),
        name="key_post",
    )(a.reshape(shape), b.reshape(shape), cos, sin)


def query_post_kernel(a_ref, b_ref, out_ref):
    out_ref[:, : REP * D] = a_ref[0]
    out_ref[:, REP * D :] = b_ref[0]


def query_post(a, b):
    source = pl.BlockSpec((1, TOK, REP * D), lambda j: (j, 0, 0))
    return pl.pallas_call(
        query_post_kernel,
        grid=(4,),
        in_specs=[source, source],
        out_specs=pl.BlockSpec((TOK, PARTS * REP * D), lambda j: (0, j)),
        out_shape=jax.ShapeDtypeStruct((TOK, HEADS * D), jnp.bfloat16),
        compiler_params=params(),
        cost_estimate=cost(1 << 20, 4 * MIB),
        name="query_post",
    )(a, b)


def project_kernel(x_ref, kg_ref, out_ref):
    nn = ((1,), (0,))
    total = dot(x_ref[0], kg_ref[0], nn)
    for i in range(1, 8):
        total += dot(x_ref[i], kg_ref[i], nn)
    out_ref[...] = total.astype(jnp.bfloat16)


def project(xt, kg):
    return pl.pallas_call(
        project_kernel,
        grid=(4,),
        in_specs=[
            pl.BlockSpec((8, 256, TOK), lambda i: (0, i, 0)),
            pl.BlockSpec((8, TOK, 512), lambda i: (0, 0, 0)),
        ],
        out_specs=pl.BlockSpec((256, 512), lambda i: (i, 0)),
        out_shape=jax.ShapeDtypeStruct((1024, 512), jnp.bfloat16),
        compiler_params=params(),
        cost_estimate=cost(10**9, 4 * MIB),
        name="project",
    )(xt, kg)


def final_sum_kernel(x_ref, out_ref):
    for c in range(2):
        total = jnp.zeros((16, 512), jnp.float32)
        for s in range(16):
            for zh in range(2):
                total += x_ref[s, c, zh].astype(jnp.float32)
        out_ref[:, c * 512 : (c + 1) * 512] = total


def final_sum(x):
    return pl.pallas_call(
        final_sum_kernel,
        in_specs=[pl.BlockSpec(memory_space=pltpu.VMEM)],
        out_specs=pl.BlockSpec(memory_space=pltpu.VMEM),
        out_shape=jax.ShapeDtypeStruct((16, 1024), jnp.float32),
        compiler_params=params(),
        cost_estimate=cost(1 << 20, MIB),
        name="final_sum",
    )(x)


def local(q, k, v, g, x, group_first, seq_length, pos_offset):
    me = lax.axis_index("sp")
    first, length, offset = group_first[0], seq_length[0], pos_offset[0]
    rates = jnp.exp(jnp.arange(HALF, dtype=jnp.float32) * (-2.0 * math.log(10000.0) / D))
    token = jnp.arange(TOK, dtype=jnp.int32)

    own = (me - first[me]) * TOK + token
    phase = (offset[me] + own).astype(jnp.float32)[:, None] * rates[None, :]
    cos, sin = jnp.cos(phase), jnp.sin(phase)
    cos = jnp.concatenate([cos, cos], -1)
    sin = jnp.concatenate([-sin, sin], -1)
    valid = jnp.broadcast_to((own < length[me]).astype(jnp.float32)[:, None], (TOK, D))

    half = me // 16
    z = me % 8 // 2
    device = half * 16 + jnp.arange(2, dtype=jnp.int32) * 8 + z * 2
    start = first[device]
    before = (device - start) * TOK
    meta = jnp.stack(
        [
            (start - half * 16) // 2,
            (device - half * 16) // 2,
            jnp.clip(length[device] - before, 0, CHUNK),
        ],
        axis=1,
    )
    place = (offset[device] + before)[:, None] + jnp.arange(CHUNK, dtype=jnp.int32)[None, :]
    turned = place.astype(jnp.float32)[:, None, :] * rates[None, :, None]
    cos_t, sin_t = jnp.cos(turned), jnp.sin(turned)

    kv_out = key_prep(k[0], v[0], cos, sin)
    qg_out = query_prep(q[0], g[0], cos, sin, valid)
    xt_out = input_prep(x[0]).reshape(8, 1024, TOK)

    dq_back, dkv_back = [], []
    arrived = []
    for part in range(PARTS):
        kv = swap(kv_out[part].reshape(16, 2, TOK, D), "sp", HALF_GROUPS)
        qg = swap(qg_out[part], "sp", QUAD_GROUPS)
        arrived.append((qg, kv))
    xt = swap(xt_out, ("sp", "dp"), Y_GROUPS)
    for qg, kv in arrived:
        dq, dkv = attention(meta, qg, kv, cos_t, sin_t)
        dkv_back.append(swap(dkv, "sp", HALF_GROUPS))
        dq_back.append(swap(dq.reshape(4, TOK, REP * D), "sp", QUAD_GROUPS))

    key_gradient, value_gradient, kg = key_post(*dkv_back, cos, sin)
    kg = swap(kg.reshape(8, TOK, 512), ("sp", "dp"), Y_GROUPS)
    partial = project(xt, kg)
    pieces = swap(partial.reshape(64, 16, 512), ("sp", "dp"), PLANE_GROUPS)
    kproj_grad = final_sum(pieces.reshape(16, 2, 2, 16, 512))
    query_grad = query_post(*dq_back)
    return (query_grad[None], key_gradient[None], value_gradient[None], kproj_grad)


def solution(mesh):
    tokens = P("dp", "sp", None)
    table = P("dp", None)
    return jax.shard_map(
        local,
        mesh=mesh,
        in_specs=(tokens,) * 5 + (table,) * 3,
        out_specs=(tokens, tokens, tokens, P(("sp", "dp"), None)),
        check_vma=False,
    )
```

```python
import math

import jax
import jax.numpy as jnp
from jax import lax
from jax.experimental import pallas as pl
from jax.experimental.pallas import tpu as pltpu
from jax.sharding import PartitionSpec as P

HEADS = 64
KV_HEADS = 8
D = 128
HALF = D // 2
TOK = 128
SP = 32
PARTS = 2
REP = HEADS // KV_HEADS
CHUNK = 2 * TOK
CHUNKS = 8
STACK = 4
ROWS = STACK * CHUNK
SCALE = D ** (-0.5)
LOG2E = 1.4426950408889634
MIB = 1 << 20

HALF_GROUPS = [list(range(16)), list(range(16, 32))]
PLANE_GROUPS = [
    [s * 8 + y * 2 + zh for s in range(SP) for zh in range(2)] for y in range(4)
]


def swap(array, axes, groups):
    return lax.all_to_all(
        array, axes, split_axis=0, concat_axis=0, axis_index_groups=groups, tiled=True
    )


def quad_send(array, delta):
    flip = (delta & 1) | (delta >> 1) << 3
    return lax.ppermute(array, "sp", [(s, s ^ flip) for s in range(SP)])


def y_send(array, step, core=0):
    pairs = []
    for s in range(SP):
        for d in range(8):
            to = ((d // 2 + step) % 4) * 2 + d % 2
            pairs.append((s * 8 + d, (s ^ core) * 8 + to))
    return lax.ppermute(array, ("sp", "dp"), pairs)


def after(array, *earlier):
    return lax.optimization_barrier((array, *earlier))[0]


def params(limit=48):
    return pltpu.CompilerParams(vmem_limit_bytes=limit * MIB)


def cost(flops, nbytes):
    return pl.CostEstimate(flops=flops, bytes_accessed=nbytes, transcendentals=0)


def dot(a, b, dims):
    return lax.dot_general(a, b, (dims, ((), ())), preferred_element_type=jnp.float32)


def turn(x, cos, sin):
    return x * cos + pltpu.roll(x, HALF, 1) * sin


def key_prep_kernel(k_ref, v_ref, cos_ref, sin_ref, *outs):
    cos, sin = cos_ref[...], sin_ref[...]
    for part in range(PARTS):
        cols = slice(part * D, (part + 1) * D)
        k = turn(k_ref[:, cols].astype(jnp.float32), cos, sin).astype(jnp.bfloat16)
        v = v_ref[:, cols]
        for z in range(4):
            outs[part][0, z, 0, 0] = k
            outs[part][0, z, 0, 1] = v


def key_prep(k, v, cos, sin):
    table = pl.BlockSpec((TOK, D), lambda j: (0, 0))
    column = pl.BlockSpec((TOK, PARTS * D), lambda j: (0, j))
    shape = jax.ShapeDtypeStruct((2, 4, 2, 2, TOK, D), jnp.bfloat16)
    return pl.pallas_call(
        key_prep_kernel,
        grid=(4,),
        in_specs=[column, column, table, table],
        out_specs=[
            pl.BlockSpec((1, 4, 1, 2, TOK, D), lambda j: (j // 2, 0, j % 2, 0, 0, 0))
        ]
        * PARTS,
        out_shape=[shape] * PARTS,
        compiler_params=params(),
        cost_estimate=cost(1 << 20, 3 * MIB),
        name="key_prep",
    )(k, v, cos, sin)


def query_prep_kernel(me_ref, q_ref, g_ref, cos_ref, sin_ref, valid_ref, *outs):
    cos, sin = cos_ref[...], sin_ref[...]
    keep = valid_ref[...] > 0.0
    for delta in range(4):

        @pl.when(pl.program_id(0) == delta)
        def _():
            for h in range(REP):
                cols = slice(h * D, (h + 1) * D)
                q = turn(q_ref[:, cols].astype(jnp.float32), cos, sin)
                outs[delta][0, :, cols] = q.astype(jnp.bfloat16)
                g = jnp.where(keep, g_ref[:, cols].astype(jnp.float32), 0.0)
                outs[delta][1, :, cols] = g.astype(jnp.bfloat16)


def query_prep(part, quad, q, g, cos, sin, valid):
    table = pl.BlockSpec((TOK, D), lambda i, me: (0, 0))
    column = pl.BlockSpec((TOK, REP * D), lambda i, me: (0, (me[0] ^ i) * PARTS + part))
    shape = jax.ShapeDtypeStruct((2, TOK, REP * D), jnp.bfloat16)
    return pl.pallas_call(
        query_prep_kernel,
        grid_spec=pltpu.PrefetchScalarGridSpec(
            num_scalar_prefetch=1,
            grid=(4,),
            in_specs=[column, column, table, table, table],
            out_specs=[pl.BlockSpec((2, TOK, REP * D), lambda i, me: (0, 0, 0))] * 4,
        ),
        out_shape=[shape] * 4,
        compiler_params=params(),
        cost_estimate=cost(4 << 20, 4 * MIB),
        name="query_prep",
    )(quad, q, g, cos, sin, valid)


def input_prep_kernel(me_ref, x_ref, *refs):
    outs, flipped = refs[:4], refs[4]
    for s in range(4):
        flipped[...] = x_ref[:, s * TOK : (s + 1) * TOK].T
        for step in range(4):
            at = pl.multiple_of((me_ref[0] + step) % 4 * 32, 32)
            outs[step][s] = flipped[pl.ds(at, 32)]


def input_prep(y, x):
    return pl.pallas_call(
        input_prep_kernel,
        grid_spec=pltpu.PrefetchScalarGridSpec(
            num_scalar_prefetch=1,
            grid=(8,),
            in_specs=[pl.BlockSpec((TOK, 512), lambda i, me: (0, i))],
            out_specs=[pl.BlockSpec((4, 32, TOK), lambda i, me: (i, 0, 0))] * 4,
            scratch_shapes=[pltpu.VMEM((TOK, TOK), jnp.bfloat16)],
        ),
        out_shape=[jax.ShapeDtypeStruct((SP, 32, TOK), jnp.bfloat16)] * 4,
        compiler_params=params(),
        cost_estimate=cost(1 << 20, 2 * MIB),
        name="input_prep",
    )(y, x)


def attention_kernel(meta_ref, *refs):
    qg_refs, (kv_ref, cos_ref, sin_ref) = refs[:4], refs[4:7]
    dq_refs, dkv_ref = refs[7:11], refs[11]
    kt_ref, e_ref, dp_ref, peak_ref, dk_ref, dv_ref, dqt_ref = refs[12:]
    heads = pl.program_id(0)
    nt, nn = ((1,), (1,)), ((1,), (0,))

    def keys(p, which):
        return kv_ref[pl.ds(2 * p, 2), which].reshape(CHUNK, D)

    @pl.when(heads == 0)
    def _():
        dk_ref[...] = jnp.zeros_like(dk_ref)
        dv_ref[...] = jnp.zeros_like(dv_ref)
        for p in range(CHUNKS):
            kt_ref[p] = keys(p, 0).T

    def attend(block):
        low, diagonal = meta_ref[block, 0], meta_ref[block, 1]
        count, core = meta_ref[block, 2], meta_ref[block, 3]

        def stacked(which):
            return jnp.concatenate(
                [
                    qg_refs[2 * block + other][which, :, h * D : (h + 1) * D]
                    for h in range(STACK)
                    for other in range(2)
                ],
                axis=0,
            )

        @pl.when(count <= 0)
        def _():
            for other in range(2):
                ref = dq_refs[2 * block + other]
                ref[...] = jnp.zeros_like(ref)

        @pl.when(count > 0)
        def _():
            q, g = stacked(0), stacked(1)

            def score(p, state, allowed=None):
                peak, total, mixed = state
                s = dot(keys(p, 0), q, nt)
                if allowed is not None:
                    s = jnp.where(allowed, s, -1e30)
                dp = dot(keys(p, 1), g, nt)
                dp_ref[p] = dp
                higher = jnp.maximum(peak, jnp.max(s, axis=0, keepdims=True))
                shrink = jnp.exp2((peak - higher) * (SCALE * LOG2E))
                e = jnp.exp2((s - higher) * (SCALE * LOG2E))
                e_ref[p] = e
                peak_ref[p] = higher
                return (
                    higher,
                    total * shrink + jnp.sum(e, axis=0, keepdims=True),
                    mixed * shrink + jnp.sum(e * dp, axis=0, keepdims=True),
                )

            zero = jnp.zeros((1, ROWS), jnp.float32)
            state = (jnp.full((1, ROWS), -1e30, jnp.float32), zero, zero)
            state = lax.fori_loop(low, diagonal, score, state)
            key_at = lax.broadcasted_iota(jnp.int32, (CHUNK, ROWS), 0)
            row_at = lax.broadcasted_iota(jnp.int32, (CHUNK, ROWS), 1) & (CHUNK - 1)
            row_at = row_at ^ (core * TOK)
            allowed = (key_at <= row_at) & (key_at < count)
            peak, total, mixed = score(diagonal, state, allowed)
            inverse = 1.0 / total
            row_dot = mixed * inverse
            dqt_ref[...] = jnp.zeros_like(dqt_ref)

            def spread(p, carry):
                factor = jnp.exp2((peak_ref[p] - peak) * (SCALE * LOG2E)) * inverse
                weights = e_ref[p] * factor
                ds = (weights * (dp_ref[p] - row_dot)).astype(jnp.bfloat16)
                dv_ref[p] += dot(weights.astype(jnp.bfloat16), g, nn)
                dk_ref[p] += dot(ds, q, nn)
                dqt_ref[...] += dot(kt_ref[p], ds, nn)
                return carry

            lax.fori_loop(low, diagonal + 1, spread, 0)
            cos, sin = cos_ref[block], sin_ref[block]
            for h in range(STACK):
                cols = slice(h * CHUNK, (h + 1) * CHUNK)
                x1 = dqt_ref[:HALF, cols] * SCALE
                x2 = dqt_ref[HALF:, cols] * SCALE
                y = jnp.concatenate([x1 * cos + x2 * sin, x2 * cos - x1 * sin], axis=0)
                y = y.T.astype(jnp.bfloat16)
                for other in range(2):
                    dq_refs[2 * block + other][:, h * D : (h + 1) * D] = y[
                        other * TOK : (other + 1) * TOK
                    ]

    attend(0)
    attend(1)

    @pl.when(heads == REP // STACK - 1)
    def _():
        for p in range(CHUNKS):
            dk = (dk_ref[p] * SCALE).astype(jnp.bfloat16)
            dkv_ref[2 * p : 2 * p + 2, 0] = dk.reshape(2, TOK, D)
            dkv_ref[2 * p : 2 * p + 2, 1] = dv_ref[p].astype(jnp.bfloat16).reshape(2, TOK, D)


def attention(meta, qg, kv, cos, sin):
    width = STACK * D
    table = pl.BlockSpec((2, HALF, CHUNK), lambda h: (0, 0, 0))
    whole = pl.BlockSpec((16, 2, TOK, D), lambda h: (0, 0, 0, 0))
    return pl.pallas_call(
        attention_kernel,
        grid=(REP // STACK,),
        in_specs=[pl.BlockSpec(memory_space=pltpu.SMEM)]
        + [pl.BlockSpec((2, TOK, width), lambda h: (0, 0, h))] * 4
        + [whole, table, table],
        out_specs=[pl.BlockSpec((TOK, width), lambda h: (0, h))] * 4 + [whole],
        out_shape=[jax.ShapeDtypeStruct((TOK, REP * D), jnp.bfloat16)] * 4
        + [jax.ShapeDtypeStruct((16, 2, TOK, D), jnp.bfloat16)],
        scratch_shapes=[
            pltpu.VMEM((CHUNKS, D, CHUNK), jnp.bfloat16),
            pltpu.VMEM((CHUNKS, CHUNK, ROWS), jnp.float32),
            pltpu.VMEM((CHUNKS, CHUNK, ROWS), jnp.float32),
            pltpu.VMEM((CHUNKS, 1, ROWS), jnp.float32),
            pltpu.VMEM((CHUNKS, CHUNK, D), jnp.float32),
            pltpu.VMEM((CHUNKS, CHUNK, D), jnp.float32),
            pltpu.VMEM((D, ROWS), jnp.float32),
        ],
        compiler_params=params(),
        cost_estimate=cost(25 * 10**9, 6 * MIB),
        name="attention",
    )(meta, *qg, kv, cos, sin)


def key_post_kernel(core_ref, in_ref, cos_ref, sin_ref, dk_ref, dv_ref, same_ref, other_ref):
    cos, sin = cos_ref[...], sin_ref[...]
    dk = in_ref[0, 0, 0, 0].astype(jnp.float32)
    dv = in_ref[0, 0, 0, 1].astype(jnp.float32)
    for z in range(1, 4):
        dk += in_ref[0, z, 0, 0].astype(jnp.float32)
        dv += in_ref[0, z, 0, 1].astype(jnp.float32)
    dk = turn(dk, cos, -sin).astype(jnp.bfloat16)
    dk_ref[0] = dk
    dv_ref[0] = dv.astype(jnp.bfloat16)
    quad = pl.program_id(0)
    for side in range(2):
        cols = slice(side * D, (side + 1) * D)

        @pl.when((quad % 2 == side) & (quad // 2 == core_ref[0]))
        def _():
            same_ref[:, cols] = dk

        @pl.when((quad % 2 == side) & (quad // 2 != core_ref[0]))
        def _():
            other_ref[:, cols] = dk


def key_post(core, back, cos, sin):
    table = pl.BlockSpec((TOK, D), lambda j, me: (0, 0))
    piece = pl.BlockSpec((TOK, 2 * D), lambda j, me: (0, 0))
    lane = pl.BlockSpec((1, TOK, D), lambda j, me: (j, 0, 0))
    full = jax.ShapeDtypeStruct((4, TOK, D), jnp.bfloat16)
    sent = jax.ShapeDtypeStruct((TOK, 2 * D), jnp.bfloat16)
    return pl.pallas_call(
        key_post_kernel,
        grid_spec=pltpu.PrefetchScalarGridSpec(
            num_scalar_prefetch=1,
            grid=(4,),
            in_specs=[
                pl.BlockSpec(
                    (1, 4, 1, 2, TOK, D), lambda j, me: (j // 2, 0, j % 2, 0, 0, 0)
                ),
                table,
                table,
            ],
            out_specs=[lane, lane, piece, piece],
        ),
        out_shape=[full, full, sent, sent],
        compiler_params=params(),
        cost_estimate=cost(1 << 20, 2 * MIB),
        name="key_post",
    )(core, back.reshape(2, 4, 2, 2, TOK, D), cos, sin)


def join_kernel(ka_ref, kb_ref, va_ref, vb_ref, dk_ref, dv_ref):
    for j in range(4):
        for part, (k_ref, v_ref) in enumerate(((ka_ref, va_ref), (kb_ref, vb_ref))):
            cols = slice((PARTS * j + part) * D, (PARTS * j + part + 1) * D)
            dk_ref[:, cols] = k_ref[j]
            dv_ref[:, cols] = v_ref[j]


def join(ka, kb, va, vb):
    vmem = pl.BlockSpec(memory_space=pltpu.VMEM)
    full = jax.ShapeDtypeStruct((TOK, KV_HEADS * D), jnp.bfloat16)
    return pl.pallas_call(
        join_kernel,
        in_specs=[vmem] * 4,
        out_specs=[vmem] * 2,
        out_shape=[full] * 2,
        compiler_params=params(),
        cost_estimate=cost(1 << 20, MIB),
        name="join",
    )(ka, kb, va, vb)


def query_post_kernel(me_ref, *refs):
    out_ref = refs[8]
    for delta in range(4):

        @pl.when(pl.program_id(0) == delta)
        def _():
            out_ref[:, : REP * D] = refs[delta][...]
            out_ref[:, REP * D :] = refs[4 + delta][...]


def query_post(quad, a, b):
    source = pl.BlockSpec((TOK, REP * D), lambda i, me: (0, 0))
    return pl.pallas_call(
        query_post_kernel,
        grid_spec=pltpu.PrefetchScalarGridSpec(
            num_scalar_prefetch=1,
            grid=(4,),
            in_specs=[source] * 8,
            out_specs=pl.BlockSpec((TOK, PARTS * REP * D), lambda i, me: (0, me[0] ^ i)),
        ),
        out_shape=jax.ShapeDtypeStruct((TOK, HEADS * D), jnp.bfloat16),
        compiler_params=params(),
        cost_estimate=cost(1 << 20, 4 * MIB),
        name="query_post",
    )(quad, *a, *b)


def project_kernel(*refs):
    nn = ((1,), (0,))
    total = dot(refs[0][...], refs[8][...], nn)
    for i in range(1, 8):
        total += dot(refs[i][...], refs[8 + i][...], nn)
    refs[16][...] = total.astype(jnp.bfloat16)


def project(xt, kg):
    return pl.pallas_call(
        project_kernel,
        grid=(2,),
        in_specs=[pl.BlockSpec((512, TOK), lambda i: (i, 0))] * 8
        + [pl.BlockSpec((TOK, 2 * D), lambda i: (0, 0))] * 8,
        out_specs=pl.BlockSpec((512, 2 * D), lambda i: (i, 0)),
        out_shape=jax.ShapeDtypeStruct((1024, 2 * D), jnp.bfloat16),
        compiler_params=params(),
        cost_estimate=cost(10**9, 3 * MIB),
        name="project",
    )(*xt, *kg)


def final_sum_kernel(a_ref, b_ref, out_ref):
    for c in range(2):
        for part, ref in enumerate((a_ref, b_ref)):
            total = jnp.zeros((16, 2 * D), jnp.float32)
            for s in range(16):
                for zh in range(2):
                    total += ref[s, c, zh].astype(jnp.float32)
            for side in range(2):
                head = (2 * c + side) * PARTS + part
                out_ref[:, head * D : (head + 1) * D] = total[:, side * D : (side + 1) * D]


def final_sum(a, b):
    vmem = pl.BlockSpec(memory_space=pltpu.VMEM)
    return pl.pallas_call(
        final_sum_kernel,
        in_specs=[vmem] * 2,
        out_specs=vmem,
        out_shape=jax.ShapeDtypeStruct((16, 1024), jnp.float32),
        compiler_params=params(),
        cost_estimate=cost(1 << 20, MIB),
        name="final_sum",
    )(a.reshape(16, 2, 2, 16, 2 * D), b.reshape(16, 2, 2, 16, 2 * D))


def local(q, k, v, g, x, group_first, seq_length, pos_offset):
    me = lax.axis_index("sp")
    first, length, offset = group_first[0], seq_length[0], pos_offset[0]
    rates = jnp.exp(jnp.arange(HALF, dtype=jnp.float32) * (-2.0 * math.log(10000.0) / D))
    token = jnp.arange(TOK, dtype=jnp.int32)

    own = (me - first[me]) * TOK + token
    phase = (offset[me] + own).astype(jnp.float32)[:, None] * rates[None, :]
    cos, sin = jnp.cos(phase), jnp.sin(phase)
    cos = jnp.concatenate([cos, cos], -1)
    sin = jnp.concatenate([-sin, sin], -1)
    valid = jnp.broadcast_to((own < length[me]).astype(jnp.float32)[:, None], (TOK, D))

    half = me // 16
    z = me % 8 // 2
    core = me % 2
    quad = me // 8 % 2 * 2 + core
    y = lax.axis_index("dp") // 2
    beside = (me // 8 % 2) ^ jnp.arange(2, dtype=jnp.int32)
    device = half * 16 + beside * 8 + z * 2
    start = first[device]
    before = (device - start) * TOK
    meta = jnp.stack(
        [
            (start - half * 16) // 2,
            (device - half * 16) // 2,
            jnp.clip(length[device] - before, 0, CHUNK),
            jnp.broadcast_to(core, (2,)),
        ],
        axis=1,
    )
    inside = jnp.arange(CHUNK, dtype=jnp.int32) ^ (core * TOK)
    place = (offset[device] + before)[:, None] + inside[None, :]
    turned = place.astype(jnp.float32)[:, None, :] * rates[None, :, None]
    cos_t, sin_t = jnp.cos(turned), jnp.sin(turned)
    quad_at, y_at, core_at = (i.astype(jnp.int32).reshape(1) for i in (quad, y, core))

    def quad_swap(pieces):
        return [pieces[0]] + [quad_send(pieces[d], d) for d in range(1, 4)]

    kv_out = [a.reshape(16, 2, TOK, D) for a in key_prep(k[0], v[0], cos, sin)]
    qg_out = [
        query_prep(part, quad_at, q[0], g[0], cos, sin, valid) for part in range(PARTS)
    ]
    qg_in = [quad_swap(qg_out[0])]
    kv_in = [swap(kv_out[0], "sp", HALF_GROUPS)]
    qg_in.append(quad_swap([after(piece, *qg_in[0]) for piece in qg_out[1]]))
    kv_in.append(swap(after(kv_out[1], kv_in[0]), "sp", HALF_GROUPS))

    xt = [a.reshape(1024, TOK) for a in input_prep(y_at, x[0])]
    xt = [xt[0]] + [y_send(xt[step], step) for step in range(1, 4)]
    xt = xt + [y_send(a, 0, 1) for a in xt]

    dq_back, dkv_back = [], []
    for part in range(PARTS):
        *dq, dkv = attention(meta, qg_in[part], kv_in[part], cos_t, sin_t)
        dkv_back.append(swap(dkv, "sp", HALF_GROUPS))
        dq_back.append(quad_swap(dq))

    dk, dv, pieces = [], [], []
    for part in range(PARTS):
        dk_part, dv_part, same, other = key_post(core_at, dkv_back[part], cos, sin)
        dk.append(dk_part)
        dv.append(dv_part)
        kg = [same] + [y_send(same, step) for step in range(1, 4)]
        kg += [y_send(other, step, 1) for step in range(4)]
        partial = project(xt, kg).reshape(64, 16, 2 * D)
        pieces.append(swap(partial, ("sp", "dp"), PLANE_GROUPS))
    kproj_grad = final_sum(*pieces)
    key_gradient, value_gradient = join(*dk, *dv)
    query_grad = query_post(quad_at, *dq_back)
    return (query_grad[None], key_gradient[None], value_gradient[None], kproj_grad)


def solution(mesh):
    tokens = P("dp", "sp", None)
    table = P("dp", None)
    return jax.shard_map(
        local,
        mesh=mesh,
        in_specs=(tokens,) * 5 + (table,) * 3,
        out_specs=(tokens, tokens, tokens, P(("sp", "dp"), None)),
        check_vma=False,
    )
```

```python
import math

import jax
import jax.numpy as jnp
from jax import lax
from jax.experimental import pallas as pl
from jax.experimental.pallas import tpu as pltpu
from jax.sharding import PartitionSpec as P

HEADS = 64
KV_HEADS = 8
D = 128
HALF = D // 2
TOK = 128
SP = 32
PARTS = 2
REP = HEADS // KV_HEADS
CHUNK = 2 * TOK
CHUNKS = 8
STACK = 4
ROWS = STACK * CHUNK
SCALE = D ** (-0.5)
LOG2E = 1.4426950408889634
MIB = 1 << 20

HALF_GROUPS = [list(range(16)), list(range(16, 32))]
PLANE_GROUPS = [
    [s * 8 + y * 2 + zh for s in range(SP) for zh in range(2)] for y in range(4)
]


def swap(array, axes, groups):
    return lax.all_to_all(
        array, axes, split_axis=0, concat_axis=0, axis_index_groups=groups, tiled=True
    )


def quad_send(array, delta):
    flip = (delta & 1) | (delta >> 1) << 3
    return lax.ppermute(array, "sp", [(s, s ^ flip) for s in range(SP)])


def y_send(array, step, core=0):
    pairs = []
    for s in range(SP):
        for d in range(8):
            to = ((d // 2 + step) % 4) * 2 + d % 2
            pairs.append((s * 8 + d, (s ^ core) * 8 + to))
    return lax.ppermute(array, ("sp", "dp"), pairs)


def after(array, *earlier):
    return lax.optimization_barrier((array, *earlier))[0]


def params(limit=12):
    return pltpu.CompilerParams(vmem_limit_bytes=limit * MIB)


def cost(flops, nbytes):
    return pl.CostEstimate(flops=flops, bytes_accessed=nbytes, transcendentals=0)


def dot(a, b, dims):
    return lax.dot_general(a, b, (dims, ((), ())), preferred_element_type=jnp.float32)


def turn(x, cos, sin):
    return x * cos + pltpu.roll(x, HALF, 1) * sin


def key_prep_kernel(k_ref, v_ref, cos_ref, sin_ref, *outs):
    cos, sin = cos_ref[...], sin_ref[...]
    for part in range(PARTS):
        cols = slice(part * D, (part + 1) * D)
        k = turn(k_ref[:, cols].astype(jnp.float32), cos, sin).astype(jnp.bfloat16)
        v = v_ref[:, cols]
        for z in range(4):
            outs[part][0, z, 0, 0] = k
            outs[part][0, z, 0, 1] = v


def key_prep(k, v, cos, sin):
    table = pl.BlockSpec((TOK, D), lambda j: (0, 0))
    column = pl.BlockSpec((TOK, PARTS * D), lambda j: (0, j))
    shape = jax.ShapeDtypeStruct((2, 4, 2, 2, TOK, D), jnp.bfloat16)
    return pl.pallas_call(
        key_prep_kernel,
        grid=(4,),
        in_specs=[column, column, table, table],
        out_specs=[
            pl.BlockSpec((1, 4, 1, 2, TOK, D), lambda j: (j // 2, 0, j % 2, 0, 0, 0))
        ]
        * PARTS,
        out_shape=[shape] * PARTS,
        compiler_params=params(),
        cost_estimate=cost(1 << 20, 3 * MIB),
        name="key_prep",
    )(k, v, cos, sin)


def query_prep_kernel(me_ref, q_ref, g_ref, cos_ref, sin_ref, valid_ref, *outs):
    cos, sin = cos_ref[...], sin_ref[...]
    keep = valid_ref[...] > 0.0
    for at, out in enumerate(outs):

        @pl.when(pl.program_id(0) == at)
        def _():
            for h in range(REP):
                cols = slice(h * D, (h + 1) * D)
                q = turn(q_ref[:, cols].astype(jnp.float32), cos, sin)
                out[0, :, cols] = q.astype(jnp.bfloat16)
                g = jnp.where(keep, g_ref[:, cols].astype(jnp.float32), 0.0)
                out[1, :, cols] = g.astype(jnp.bfloat16)


def query_prep(part, deltas, quad, q, g, cos, sin, valid):
    count, low = len(deltas), deltas[0]
    first = part == 0 and low == 1
    table = pl.BlockSpec((TOK, D), lambda i, me: (0, 0))
    column = pl.BlockSpec(
        (TOK, REP * D), lambda i, me: (0, (me[0] ^ (i + low)) * PARTS + part)
    )
    shape = jax.ShapeDtypeStruct((2, TOK, REP * D), jnp.bfloat16)
    return pl.pallas_call(
        query_prep_kernel,
        grid_spec=pltpu.PrefetchScalarGridSpec(
            num_scalar_prefetch=1,
            grid=(count,),
            in_specs=[column, column, table, table, table],
            out_specs=[pl.BlockSpec((2, TOK, REP * D), lambda i, me: (0, 0, 0))] * count,
        ),
        out_shape=[shape] * count,
        compiler_params=params(56 if first else 12),
        cost_estimate=cost(count << 20, count * MIB),
        name="query_prep",
    )(quad, q, g, cos, sin, valid)


def input_prep_kernel(me_ref, x_ref, *refs):
    outs, flipped = refs[:4], refs[4]
    for s in range(4):
        flipped[...] = x_ref[:, s * TOK : (s + 1) * TOK].T
        for step in range(4):
            at = pl.multiple_of((me_ref[0] + step) % 4 * 32, 32)
            outs[step][s] = flipped[pl.ds(at, 32)]


def input_prep(y, x):
    return pl.pallas_call(
        input_prep_kernel,
        grid_spec=pltpu.PrefetchScalarGridSpec(
            num_scalar_prefetch=1,
            grid=(8,),
            in_specs=[pl.BlockSpec((TOK, 512), lambda i, me: (0, i))],
            out_specs=[pl.BlockSpec((4, 32, TOK), lambda i, me: (i, 0, 0))] * 4,
            scratch_shapes=[pltpu.VMEM((TOK, TOK), jnp.bfloat16)],
        ),
        out_shape=[jax.ShapeDtypeStruct((SP, 32, TOK), jnp.bfloat16)] * 4,
        compiler_params=params(),
        cost_estimate=cost(1 << 20, 2 * MIB),
        name="input_prep",
    )(y, x)


def attention_kernel(meta_ref, *refs):
    qg_refs, (kv_ref, cos_ref, sin_ref) = refs[:4], refs[4:7]
    dq_refs, dkv_ref = refs[7:11], refs[11]
    kt_ref, e_ref, dp_ref, peak_ref, dk_ref, dv_ref, dqt_ref = refs[12:]
    heads = pl.program_id(0)
    nt, nn = ((1,), (1,)), ((1,), (0,))

    def keys(p, which):
        return kv_ref[pl.ds(2 * p, 2), which].reshape(CHUNK, D)

    @pl.when(heads == 0)
    def _():
        dk_ref[...] = jnp.zeros_like(dk_ref)
        dv_ref[...] = jnp.zeros_like(dv_ref)
        for p in range(CHUNKS):
            kt_ref[p] = keys(p, 0).T

    def attend(block):
        low, diagonal = meta_ref[block, 0], meta_ref[block, 1]
        count, core = meta_ref[block, 2], meta_ref[block, 3]

        def stacked(which):
            return jnp.concatenate(
                [
                    qg_refs[2 * block + other][which, :, h * D : (h + 1) * D]
                    for h in range(STACK)
                    for other in range(2)
                ],
                axis=0,
            )

        @pl.when(count <= 0)
        def _():
            for other in range(2):
                ref = dq_refs[2 * block + other]
                ref[...] = jnp.zeros_like(ref)

        @pl.when(count > 0)
        def _():
            q, g = stacked(0), stacked(1)

            def score(p, state, allowed=None):
                peak, total, mixed = state
                s = dot(keys(p, 0), q, nt)
                if allowed is not None:
                    s = jnp.where(allowed, s, -1e30)
                dp = dot(keys(p, 1), g, nt)
                dp_ref[p] = dp
                higher = jnp.maximum(peak, jnp.max(s, axis=0, keepdims=True))
                shrink = jnp.exp2((peak - higher) * (SCALE * LOG2E))
                e = jnp.exp2((s - higher) * (SCALE * LOG2E))
                e_ref[p] = e
                peak_ref[p] = higher
                return (
                    higher,
                    total * shrink + jnp.sum(e, axis=0, keepdims=True),
                    mixed * shrink + jnp.sum(e * dp, axis=0, keepdims=True),
                )

            zero = jnp.zeros((1, ROWS), jnp.float32)
            state = (jnp.full((1, ROWS), -1e30, jnp.float32), zero, zero)
            state = lax.fori_loop(low, diagonal, score, state)
            key_at = lax.broadcasted_iota(jnp.int32, (CHUNK, ROWS), 0)
            row_at = lax.broadcasted_iota(jnp.int32, (CHUNK, ROWS), 1) & (CHUNK - 1)
            row_at = row_at ^ (core * TOK)
            allowed = (key_at <= row_at) & (key_at < count)
            peak, total, mixed = score(diagonal, state, allowed)
            inverse = 1.0 / total
            row_dot = mixed * inverse
            dqt_ref[...] = jnp.zeros_like(dqt_ref)

            def spread(p, carry):
                factor = jnp.exp2((peak_ref[p] - peak) * (SCALE * LOG2E)) * inverse
                weights = e_ref[p] * factor
                ds = (weights * (dp_ref[p] - row_dot)).astype(jnp.bfloat16)
                dv_ref[p] += dot(weights.astype(jnp.bfloat16), g, nn)
                dk_ref[p] += dot(ds, q, nn)
                dqt_ref[...] += dot(kt_ref[p], ds, nn)
                return carry

            lax.fori_loop(low, diagonal + 1, spread, 0)
            cos, sin = cos_ref[block], sin_ref[block]
            for h in range(STACK):
                cols = slice(h * CHUNK, (h + 1) * CHUNK)
                x1 = dqt_ref[:HALF, cols] * SCALE
                x2 = dqt_ref[HALF:, cols] * SCALE
                y = jnp.concatenate([x1 * cos + x2 * sin, x2 * cos - x1 * sin], axis=0)
                y = y.T.astype(jnp.bfloat16)
                for other in range(2):
                    dq_refs[2 * block + other][:, h * D : (h + 1) * D] = y[
                        other * TOK : (other + 1) * TOK
                    ]

    attend(0)
    attend(1)

    @pl.when(heads == REP // STACK - 1)
    def _():
        for p in range(CHUNKS):
            dk = (dk_ref[p] * SCALE).astype(jnp.bfloat16)
            dkv_ref[2 * p : 2 * p + 2, 0] = dk.reshape(2, TOK, D)
            dkv_ref[2 * p : 2 * p + 2, 1] = dv_ref[p].astype(jnp.bfloat16).reshape(2, TOK, D)


def attention(meta, qg, kv, cos, sin):
    width = STACK * D
    table = pl.BlockSpec((2, HALF, CHUNK), lambda h: (0, 0, 0))
    whole = pl.BlockSpec((16, 2, TOK, D), lambda h: (0, 0, 0, 0))
    return pl.pallas_call(
        attention_kernel,
        grid=(REP // STACK,),
        in_specs=[pl.BlockSpec(memory_space=pltpu.SMEM)]
        + [pl.BlockSpec((2, TOK, width), lambda h: (0, 0, h))] * 4
        + [whole, table, table],
        out_specs=[pl.BlockSpec((TOK, width), lambda h: (0, h))] * 4 + [whole],
        out_shape=[jax.ShapeDtypeStruct((TOK, REP * D), jnp.bfloat16)] * 4
        + [jax.ShapeDtypeStruct((16, 2, TOK, D), jnp.bfloat16)],
        scratch_shapes=[
            pltpu.VMEM((CHUNKS, D, CHUNK), jnp.bfloat16),
            pltpu.VMEM((CHUNKS, CHUNK, ROWS), jnp.float32),
            pltpu.VMEM((CHUNKS, CHUNK, ROWS), jnp.float32),
            pltpu.VMEM((CHUNKS, 1, ROWS), jnp.float32),
            pltpu.VMEM((CHUNKS, CHUNK, D), jnp.float32),
            pltpu.VMEM((CHUNKS, CHUNK, D), jnp.float32),
            pltpu.VMEM((D, ROWS), jnp.float32),
        ],
        compiler_params=params(34),
        cost_estimate=cost(25 * 10**9, 6 * MIB),
        name="attention",
    )(meta, *qg, kv, cos, sin)


def key_post_kernel(core_ref, in_ref, cos_ref, sin_ref, dk_ref, dv_ref, same_ref, other_ref):
    cos, sin = cos_ref[...], sin_ref[...]
    dk = in_ref[0, 0, 0, 0].astype(jnp.float32)
    dv = in_ref[0, 0, 0, 1].astype(jnp.float32)
    for z in range(1, 4):
        dk += in_ref[0, z, 0, 0].astype(jnp.float32)
        dv += in_ref[0, z, 0, 1].astype(jnp.float32)
    dk = turn(dk, cos, -sin).astype(jnp.bfloat16)
    dk_ref[0] = dk
    dv_ref[0] = dv.astype(jnp.bfloat16)
    quad = pl.program_id(0)
    for side in range(2):
        cols = slice(side * D, (side + 1) * D)

        @pl.when((quad % 2 == side) & (quad // 2 == core_ref[0]))
        def _():
            same_ref[:, cols] = dk

        @pl.when((quad % 2 == side) & (quad // 2 != core_ref[0]))
        def _():
            other_ref[:, cols] = dk


def key_post(core, back, cos, sin):
    table = pl.BlockSpec((TOK, D), lambda j, me: (0, 0))
    piece = pl.BlockSpec((TOK, 2 * D), lambda j, me: (0, 0))
    lane = pl.BlockSpec((1, TOK, D), lambda j, me: (j, 0, 0))
    full = jax.ShapeDtypeStruct((4, TOK, D), jnp.bfloat16)
    sent = jax.ShapeDtypeStruct((TOK, 2 * D), jnp.bfloat16)
    return pl.pallas_call(
        key_post_kernel,
        grid_spec=pltpu.PrefetchScalarGridSpec(
            num_scalar_prefetch=1,
            grid=(4,),
            in_specs=[
                pl.BlockSpec(
                    (1, 4, 1, 2, TOK, D), lambda j, me: (j // 2, 0, j % 2, 0, 0, 0)
                ),
                table,
                table,
            ],
            out_specs=[lane, lane, piece, piece],
        ),
        out_shape=[full, full, sent, sent],
        compiler_params=params(),
        cost_estimate=cost(1 << 20, 2 * MIB),
        name="key_post",
    )(core, back.reshape(2, 4, 2, 2, TOK, D), cos, sin)


def join_kernel(ka_ref, kb_ref, va_ref, vb_ref, dk_ref, dv_ref):
    for j in range(4):
        for part, (k_ref, v_ref) in enumerate(((ka_ref, va_ref), (kb_ref, vb_ref))):
            cols = slice((PARTS * j + part) * D, (PARTS * j + part + 1) * D)
            dk_ref[:, cols] = k_ref[j]
            dv_ref[:, cols] = v_ref[j]


def join(ka, kb, va, vb):
    vmem = pl.BlockSpec(memory_space=pltpu.VMEM)
    full = jax.ShapeDtypeStruct((TOK, KV_HEADS * D), jnp.bfloat16)
    return pl.pallas_call(
        join_kernel,
        in_specs=[vmem] * 4,
        out_specs=[vmem] * 2,
        out_shape=[full] * 2,
        compiler_params=params(),
        cost_estimate=cost(1 << 20, MIB),
        name="join",
    )(ka, kb, va, vb)


def query_post_kernel(me_ref, *refs):
    out_ref = refs[8]
    for delta in range(4):

        @pl.when(pl.program_id(0) == delta)
        def _():
            out_ref[:, : REP * D] = refs[delta][...]
            out_ref[:, REP * D :] = refs[4 + delta][...]


def query_post(quad, a, b):
    source = pl.BlockSpec((TOK, REP * D), lambda i, me: (0, 0))
    return pl.pallas_call(
        query_post_kernel,
        grid_spec=pltpu.PrefetchScalarGridSpec(
            num_scalar_prefetch=1,
            grid=(4,),
            in_specs=[source] * 8,
            out_specs=pl.BlockSpec((TOK, PARTS * REP * D), lambda i, me: (0, me[0] ^ i)),
        ),
        out_shape=jax.ShapeDtypeStruct((TOK, HEADS * D), jnp.bfloat16),
        compiler_params=params(),
        cost_estimate=cost(1 << 20, 4 * MIB),
        name="query_post",
    )(quad, *a, *b)


def project_kernel(*refs):
    nn = ((1,), (0,))
    total = dot(refs[0][...], refs[8][...], nn)
    for i in range(1, 8):
        total += dot(refs[i][...], refs[8 + i][...], nn)
    total = total.astype(jnp.bfloat16)
    if len(refs) == 17:
        refs[16][...] = total
    else:
        refs[17][:, : 2 * D] = refs[16][...]
        refs[17][:, 2 * D :] = total


def project(xt, kg, earlier=()):
    width = 2 * D * (1 + len(earlier))
    return pl.pallas_call(
        project_kernel,
        grid=(2,),
        in_specs=[pl.BlockSpec((512, TOK), lambda i: (i, 0))] * 8
        + [pl.BlockSpec((TOK, 2 * D), lambda i: (0, 0))] * 8
        + [pl.BlockSpec((512, 2 * D), lambda i: (i, 0))] * len(earlier),
        out_specs=pl.BlockSpec((512, width), lambda i: (i, 0)),
        out_shape=jax.ShapeDtypeStruct((1024, width), jnp.bfloat16),
        compiler_params=params(),
        cost_estimate=cost(10**9, 3 * MIB),
        name="project",
    )(*xt, *kg, *earlier)


def final_sum_kernel(in_ref, out_ref):
    for c in range(2):
        total = jnp.zeros((16, PARTS * 2 * D), jnp.float32)
        for s in range(16):
            for zh in range(2):
                total += in_ref[s, c, zh].astype(jnp.float32)
        for part in range(PARTS):
            for side in range(2):
                head = (2 * c + side) * PARTS + part
                at = (part * 2 + side) * D
                out_ref[:, head * D : (head + 1) * D] = total[:, at : at + D]


def final_sum(pieces):
    vmem = pl.BlockSpec(memory_space=pltpu.VMEM)
    return pl.pallas_call(
        final_sum_kernel,
        in_specs=[vmem],
        out_specs=vmem,
        out_shape=jax.ShapeDtypeStruct((16, 1024), jnp.float32),
        compiler_params=params(),
        cost_estimate=cost(1 << 20, MIB),
        name="final_sum",
    )(pieces.reshape(16, 2, 2, 16, PARTS * 2 * D))


def local(q, k, v, g, x, group_first, seq_length, pos_offset):
    me = lax.axis_index("sp")
    first, length, offset = group_first[0], seq_length[0], pos_offset[0]
    rates = jnp.exp(jnp.arange(HALF, dtype=jnp.float32) * (-2.0 * math.log(10000.0) / D))
    token = jnp.arange(TOK, dtype=jnp.int32)

    own = (me - first[me]) * TOK + token
    phase = (offset[me] + own).astype(jnp.float32)[:, None] * rates[None, :]
    cos, sin = jnp.cos(phase), jnp.sin(phase)
    cos = jnp.concatenate([cos, cos], -1)
    sin = jnp.concatenate([-sin, sin], -1)
    valid = jnp.broadcast_to((own < length[me]).astype(jnp.float32)[:, None], (TOK, D))

    half = me // 16
    z = me % 8 // 2
    core = me % 2
    quad = me // 8 % 2 * 2 + core
    y = lax.axis_index("dp") // 2
    beside = (me // 8 % 2) ^ jnp.arange(2, dtype=jnp.int32)
    device = half * 16 + beside * 8 + z * 2
    start = first[device]
    before = (device - start) * TOK
    meta = jnp.stack(
        [
            (start - half * 16) // 2,
            (device - half * 16) // 2,
            jnp.clip(length[device] - before, 0, CHUNK),
            jnp.broadcast_to(core, (2,)),
        ],
        axis=1,
    )
    inside = jnp.arange(CHUNK, dtype=jnp.int32) ^ (core * TOK)
    place = (offset[device] + before)[:, None] + inside[None, :]
    turned = place.astype(jnp.float32)[:, None, :] * rates[None, :, None]
    cos_t, sin_t = jnp.cos(turned), jnp.sin(turned)
    quad_at, y_at, core_at = (i.astype(jnp.int32).reshape(1) for i in (quad, y, core))

    def quad_swap(pieces):
        return [pieces[0]] + [quad_send(pieces[d], d) for d in range(1, 4)]

    def query_pieces(part, deltas):
        return query_prep(part, deltas, quad_at, q[0], g[0], cos, sin, valid)

    def quad_swap(pieces):
        return [quad_send(piece, d + 1) for d, piece in enumerate(pieces)]

    sent = query_pieces(0, (1, 2, 3))
    qg_in = [quad_swap(sent)]
    kv_out = key_prep(after(k[0], *sent), v[0], cos, sin)
    kv_out = [a.reshape(16, 2, TOK, D) for a in kv_out]
    kv_in = [swap(kv_out[0], "sp", HALF_GROUPS)]
    xt = [a.reshape(1024, TOK) for a in input_prep(y_at, after(x[0], qg_in[0][0]))]
    xt = [xt[0]] + [y_send(xt[step], step) for step in range(1, 4)]
    qg_in[0] = list(query_pieces(0, (0,))) + qg_in[0]
    kv_in[0] = after(kv_in[0], *xt)

    own = query_pieces(1, (0,))
    sent = query_pieces(1, (1, 2, 3))
    qg_in.append(list(own) + quad_swap([after(piece, *qg_in[0]) for piece in sent]))
    kv_in.append(swap(after(kv_out[1], kv_in[0]), "sp", HALF_GROUPS))
    xt = xt + [y_send(a, 0, 1) for a in xt]
    kv_in[1] = after(kv_in[1], *xt)

    dq_back, dkv_back = [], []
    for part in range(PARTS):
        *dq, dkv = attention(meta, qg_in[part], kv_in[part], cos_t, sin_t)
        dkv_back.append(swap(dkv, "sp", HALF_GROUPS))
        dq_back.append([dq[0]] + quad_swap(dq[1:]))

    dk, dv, partial = [], [], ()
    for part in range(PARTS):
        back = after(dkv_back[part], *dq_back[part])
        dk_part, dv_part, same, other = key_post(core_at, back, cos, sin)
        dk.append(dk_part)
        dv.append(dv_part)
        kg = [same] + [y_send(same, step) for step in range(1, 4)]
        kg += [y_send(other, step, 1) for step in range(4)]
        partial = (project(xt, kg, partial),)
    pieces = swap(partial[0].reshape(64, 16, 4 * D), ("sp", "dp"), PLANE_GROUPS)
    kproj_grad = final_sum(pieces)
    key_gradient, value_gradient = join(*dk, *dv)
    query_grad = query_post(quad_at, *dq_back)
    return (query_grad[None], key_gradient[None], value_gradient[None], kproj_grad)


def solution(mesh):
    tokens = P("dp", "sp", None)
    table = P("dp", None)
    return jax.shard_map(
        local,
        mesh=mesh,
        in_specs=(tokens,) * 5 + (table,) * 3,
        out_specs=(tokens, tokens, tokens, P(("sp", "dp"), None)),
        check_vma=False,
    )
```

```python
import math

import jax
import jax.numpy as jnp
from jax import lax
from jax.experimental import pallas as pl
from jax.experimental.pallas import tpu as pltpu
from jax.sharding import PartitionSpec as P

HEADS = 64
KV_HEADS = 8
D = 128
HALF = D // 2
TOK = 128
SP = 32
PARTS = 2
REP = HEADS // KV_HEADS
CHUNK = 2 * TOK
CHUNKS = 8
STACK = 4
ROWS = STACK * CHUNK
SCALE = D ** (-0.5)
LOG2E = 1.4426950408889634
MIB = 1 << 20

HALF_GROUPS = [list(range(16)), list(range(16, 32))]
PLANE_GROUPS = [
    [s * 8 + y * 2 + zh for s in range(SP) for zh in range(2)] for y in range(4)
]


def swap(array, axes, groups):
    return lax.all_to_all(
        array, axes, split_axis=0, concat_axis=0, axis_index_groups=groups, tiled=True
    )


def quad_send(array, delta):
    flip = (delta & 1) | (delta >> 1) << 3
    return lax.ppermute(array, "sp", [(s, s ^ flip) for s in range(SP)])


def y_send(array, step, core=0):
    pairs = []
    for s in range(SP):
        for d in range(8):
            to = ((d // 2 + step) % 4) * 2 + d % 2
            pairs.append((s * 8 + d, (s ^ core) * 8 + to))
    return lax.ppermute(array, ("sp", "dp"), pairs)


def after(array, *earlier):
    return lax.optimization_barrier((array, *earlier))[0]


def params(limit=12):
    return pltpu.CompilerParams(vmem_limit_bytes=limit * MIB)


def cost(flops, nbytes):
    return pl.CostEstimate(flops=flops, bytes_accessed=nbytes, transcendentals=0)


def dot(a, b, dims):
    return lax.dot_general(a, b, (dims, ((), ())), preferred_element_type=jnp.float32)


def turn(x, cos, sin):
    return x * cos + pltpu.roll(x, HALF, 1) * sin


def key_send_kernel(k_ref, v_ref, *outs):
    for part in range(PARTS):
        cols = slice(part * D, (part + 1) * D)
        for z in range(4):
            outs[part][0, z, 0, 0] = k_ref[:, cols]
            outs[part][0, z, 0, 1] = v_ref[:, cols]


def key_send(k, v):
    column = pl.BlockSpec((TOK, PARTS * D), lambda j: (0, j))
    shape = jax.ShapeDtypeStruct((2, 4, 2, 2, TOK, D), jnp.bfloat16)
    return pl.pallas_call(
        key_send_kernel,
        grid=(4,),
        in_specs=[column, column],
        out_specs=[
            pl.BlockSpec((1, 4, 1, 2, TOK, D), lambda j: (j // 2, 0, j % 2, 0, 0, 0))
        ]
        * PARTS,
        out_shape=[shape] * PARTS,
        compiler_params=params(56),
        cost_estimate=cost(1 << 20, 3 * MIB),
        name="key_send",
    )(k, v)


def key_turn_kernel(kv_ref, cos_ref, sin_ref, k_ref, kt_ref, v_ref):
    for half in range(2):
        rows = slice(half * TOK, (half + 1) * TOK)
        k = kv_ref[half, 0].astype(jnp.float32)
        k = turn(k, cos_ref[0, rows], sin_ref[0, rows]).astype(jnp.bfloat16)
        k_ref[0, rows] = k
        kt_ref[0, :, rows] = k.T
        v_ref[0, rows] = kv_ref[half, 1]


def key_turn(kv, cos, sin):
    rows = pl.BlockSpec((1, CHUNK, D), lambda p: (p, 0, 0))
    shape = jax.ShapeDtypeStruct((CHUNKS, CHUNK, D), jnp.bfloat16)
    return pl.pallas_call(
        key_turn_kernel,
        grid=(CHUNKS,),
        in_specs=[
            pl.BlockSpec((2, 2, TOK, D), lambda p: (p, 0, 0, 0)),
            rows,
            rows,
        ],
        out_specs=[rows, pl.BlockSpec((1, D, CHUNK), lambda p: (p, 0, 0)), rows],
        out_shape=[shape, jax.ShapeDtypeStruct((CHUNKS, D, CHUNK), jnp.bfloat16), shape],
        compiler_params=params(),
        cost_estimate=cost(1 << 20, 4 * MIB),
        name="key_turn",
    )(kv, cos, sin)


def query_prep_kernel(me_ref, q_ref, g_ref, cos_ref, sin_ref, valid_ref, *outs):
    cos, sin = cos_ref[...], sin_ref[...]
    keep = valid_ref[...] > 0.0
    for at, out in enumerate(outs):

        @pl.when(pl.program_id(0) == at)
        def _():
            for h in range(REP):
                cols = slice(h * D, (h + 1) * D)
                q = turn(q_ref[:, cols].astype(jnp.float32), cos, sin)
                out[0, :, cols] = q.astype(jnp.bfloat16)
                g = jnp.where(keep, g_ref[:, cols].astype(jnp.float32), 0.0)
                out[1, :, cols] = g.astype(jnp.bfloat16)


def query_prep(part, deltas, quad, q, g, cos, sin, valid):
    count, low = len(deltas), deltas[0]
    first = part == 0 and low == 1
    table = pl.BlockSpec((TOK, D), lambda i, me: (0, 0))
    column = pl.BlockSpec(
        (TOK, REP * D), lambda i, me: (0, (me[0] ^ (i + low)) * PARTS + part)
    )
    shape = jax.ShapeDtypeStruct((2, TOK, REP * D), jnp.bfloat16)
    return pl.pallas_call(
        query_prep_kernel,
        grid_spec=pltpu.PrefetchScalarGridSpec(
            num_scalar_prefetch=1,
            grid=(count,),
            in_specs=[column, column, table, table, table],
            out_specs=[pl.BlockSpec((2, TOK, REP * D), lambda i, me: (0, 0, 0))] * count,
        ),
        out_shape=[shape] * count,
        compiler_params=params(56 if first else 12),
        cost_estimate=cost(count << 20, count * MIB),
        name="query_prep",
    )(quad, q, g, cos, sin, valid)


def input_prep_kernel(me_ref, x_ref, *refs):
    outs, flipped = refs[:4], refs[4]
    for s in range(4):
        flipped[...] = x_ref[:, s * TOK : (s + 1) * TOK].T
        for step in range(4):
            at = pl.multiple_of((me_ref[0] + step) % 4 * 32, 32)
            outs[step][s] = flipped[pl.ds(at, 32)]


def input_prep(y, x):
    return pl.pallas_call(
        input_prep_kernel,
        grid_spec=pltpu.PrefetchScalarGridSpec(
            num_scalar_prefetch=1,
            grid=(8,),
            in_specs=[pl.BlockSpec((TOK, 512), lambda i, me: (0, i))],
            out_specs=[pl.BlockSpec((4, 32, TOK), lambda i, me: (i, 0, 0))] * 4,
            scratch_shapes=[pltpu.VMEM((TOK, TOK), jnp.bfloat16)],
        ),
        out_shape=[jax.ShapeDtypeStruct((SP, 32, TOK), jnp.bfloat16)] * 4,
        compiler_params=params(),
        cost_estimate=cost(1 << 20, 2 * MIB),
        name="input_prep",
    )(y, x)


def attention_kernel(meta_ref, *refs):
    qg_refs, (k_ref, kt_ref, v_ref, cos_ref, sin_ref) = refs[:4], refs[4:9]
    dq_refs, dkv_ref = refs[9:13], refs[13]
    e_ref, dp_ref, peak_ref, dk_ref, dv_ref, dqt_ref = refs[14:]
    heads = pl.program_id(0)
    nt, nn = ((1,), (1,)), ((1,), (0,))

    @pl.when(heads == 0)
    def _():
        dk_ref[...] = jnp.zeros_like(dk_ref)
        dv_ref[...] = jnp.zeros_like(dv_ref)

    def attend(block):
        low, diagonal = meta_ref[block, 0], meta_ref[block, 1]
        count, core = meta_ref[block, 2], meta_ref[block, 3]

        def stacked(which):
            return jnp.concatenate(
                [
                    qg_refs[2 * block + other][which, :, h * D : (h + 1) * D]
                    for h in range(STACK)
                    for other in range(2)
                ],
                axis=0,
            )

        @pl.when(count <= 0)
        def _():
            for other in range(2):
                ref = dq_refs[2 * block + other]
                ref[...] = jnp.zeros_like(ref)

        @pl.when(count > 0)
        def _():
            q, g = stacked(0), stacked(1)
            columns = [slice(h * CHUNK, (h + 1) * CHUNK) for h in range(STACK)]

            def score(p, state, allowed=None):
                k, v = k_ref[p], v_ref[p]
                after = []
                for cols, (peak, total, mixed) in zip(columns, state):
                    s = dot(k, q[cols], nt)
                    if allowed is not None:
                        s = jnp.where(allowed, s, -1e30)
                    dp = dot(v, g[cols], nt)
                    dp_ref[p, :, cols] = dp
                    higher = jnp.maximum(peak, jnp.max(s, axis=0, keepdims=True))
                    shrink = jnp.exp2((peak - higher) * (SCALE * LOG2E))
                    e = jnp.exp2((s - higher) * (SCALE * LOG2E))
                    e_ref[p, :, cols] = e
                    peak_ref[p, :, cols] = higher
                    total = total * shrink + jnp.sum(e, axis=0, keepdims=True)
                    mixed = mixed * shrink + jnp.sum(e * dp, axis=0, keepdims=True)
                    after.append((higher, total, mixed))
                return tuple(after)

            zero = jnp.zeros((1, CHUNK), jnp.float32)
            state = ((jnp.full((1, CHUNK), -1e30, jnp.float32), zero, zero),) * STACK
            state = lax.fori_loop(low, diagonal, score, state)
            key_at = lax.broadcasted_iota(jnp.int32, (CHUNK, CHUNK), 0)
            row_at = lax.broadcasted_iota(jnp.int32, (CHUNK, CHUNK), 1) ^ (core * TOK)
            allowed = (key_at <= row_at) & (key_at < count)
            state = score(diagonal, state, allowed)
            final = []
            for peak, total, mixed in state:
                inverse = 1.0 / total
                final.append((peak, inverse, mixed * inverse))
            dqt_ref[...] = jnp.zeros_like(dqt_ref)

            def spread(p, carry):
                kt = kt_ref[p]
                rounded, grads = [], []
                for cols, (peak, inverse, row_dot) in zip(columns, final):
                    factor = jnp.exp2((peak_ref[p, :, cols] - peak) * (SCALE * LOG2E))
                    weights = e_ref[p, :, cols] * (factor * inverse)
                    ds = (weights * (dp_ref[p, :, cols] - row_dot)).astype(jnp.bfloat16)
                    rounded.append(weights.astype(jnp.bfloat16))
                    grads.append(ds)
                    dqt_ref[:, cols] += dot(kt, ds, nn)
                dv_ref[p] += dot(jnp.concatenate(rounded, axis=1), g, nn)
                dk_ref[p] += dot(jnp.concatenate(grads, axis=1), q, nn)
                return carry

            lax.fori_loop(low, diagonal + 1, spread, 0)
            cos, sin = cos_ref[block], sin_ref[block]
            for h in range(STACK):
                cols = slice(h * CHUNK, (h + 1) * CHUNK)
                x1 = dqt_ref[:HALF, cols] * SCALE
                x2 = dqt_ref[HALF:, cols] * SCALE
                y = jnp.concatenate([x1 * cos + x2 * sin, x2 * cos - x1 * sin], axis=0)
                y = y.T.astype(jnp.bfloat16)
                for other in range(2):
                    dq_refs[2 * block + other][:, h * D : (h + 1) * D] = y[
                        other * TOK : (other + 1) * TOK
                    ]

    attend(0)
    attend(1)

    @pl.when(heads == REP // STACK - 1)
    def _():
        for p in range(CHUNKS):
            dk = (dk_ref[p] * SCALE).astype(jnp.bfloat16)
            dkv_ref[2 * p : 2 * p + 2, 0] = dk.reshape(2, TOK, D)
            dkv_ref[2 * p : 2 * p + 2, 1] = dv_ref[p].astype(jnp.bfloat16).reshape(2, TOK, D)


def attention(meta, qg, keys, cos, sin):
    width = STACK * D
    table = pl.BlockSpec((2, HALF, CHUNK), lambda h: (0, 0, 0))
    stacked = pl.BlockSpec((CHUNKS, CHUNK, D), lambda h: (0, 0, 0))
    turned = pl.BlockSpec((CHUNKS, D, CHUNK), lambda h: (0, 0, 0))
    whole = pl.BlockSpec((16, 2, TOK, D), lambda h: (0, 0, 0, 0))
    return pl.pallas_call(
        attention_kernel,
        grid=(REP // STACK,),
        in_specs=[pl.BlockSpec(memory_space=pltpu.SMEM)]
        + [pl.BlockSpec((2, TOK, width), lambda h: (0, 0, h))] * 4
        + [stacked, turned, stacked, table, table],
        out_specs=[pl.BlockSpec((TOK, width), lambda h: (0, h))] * 4 + [whole],
        out_shape=[jax.ShapeDtypeStruct((TOK, REP * D), jnp.bfloat16)] * 4
        + [jax.ShapeDtypeStruct((16, 2, TOK, D), jnp.bfloat16)],
        scratch_shapes=[
            pltpu.VMEM((CHUNKS, CHUNK, ROWS), jnp.float32),
            pltpu.VMEM((CHUNKS, CHUNK, ROWS), jnp.float32),
            pltpu.VMEM((CHUNKS, 1, ROWS), jnp.float32),
            pltpu.VMEM((CHUNKS, CHUNK, D), jnp.float32),
            pltpu.VMEM((CHUNKS, CHUNK, D), jnp.float32),
            pltpu.VMEM((D, ROWS), jnp.float32),
        ],
        compiler_params=params(34),
        cost_estimate=cost(25 * 10**9, 6 * MIB),
        name="attention",
    )(meta, *qg, *keys, cos, sin)


def key_post_kernel(core_ref, in_ref, cos_ref, sin_ref, dk_ref, dv_ref, same_ref, other_ref):
    cos, sin = cos_ref[...], sin_ref[...]
    dk = in_ref[0, 0, 0, 0].astype(jnp.float32)
    dv = in_ref[0, 0, 0, 1].astype(jnp.float32)
    for z in range(1, 4):
        dk += in_ref[0, z, 0, 0].astype(jnp.float32)
        dv += in_ref[0, z, 0, 1].astype(jnp.float32)
    dk = turn(dk, cos, -sin).astype(jnp.bfloat16)
    dk_ref[0] = dk
    dv_ref[0] = dv.astype(jnp.bfloat16)
    quad = pl.program_id(0)
    for side in range(2):
        cols = slice(side * D, (side + 1) * D)

        @pl.when((quad % 2 == side) & (quad // 2 == core_ref[0]))
        def _():
            same_ref[:, cols] = dk

        @pl.when((quad % 2 == side) & (quad // 2 != core_ref[0]))
        def _():
            other_ref[:, cols] = dk


def key_post(core, back, cos, sin):
    table = pl.BlockSpec((TOK, D), lambda j, me: (0, 0))
    piece = pl.BlockSpec((TOK, 2 * D), lambda j, me: (0, 0))
    lane = pl.BlockSpec((1, TOK, D), lambda j, me: (j, 0, 0))
    full = jax.ShapeDtypeStruct((4, TOK, D), jnp.bfloat16)
    sent = jax.ShapeDtypeStruct((TOK, 2 * D), jnp.bfloat16)
    return pl.pallas_call(
        key_post_kernel,
        grid_spec=pltpu.PrefetchScalarGridSpec(
            num_scalar_prefetch=1,
            grid=(4,),
            in_specs=[
                pl.BlockSpec(
                    (1, 4, 1, 2, TOK, D), lambda j, me: (j // 2, 0, j % 2, 0, 0, 0)
                ),
                table,
                table,
            ],
            out_specs=[lane, lane, piece, piece],
        ),
        out_shape=[full, full, sent, sent],
        compiler_params=params(),
        cost_estimate=cost(1 << 20, 2 * MIB),
        name="key_post",
    )(core, back.reshape(2, 4, 2, 2, TOK, D), cos, sin)


def join_kernel(ka_ref, kb_ref, va_ref, vb_ref, dk_ref, dv_ref):
    for j in range(4):
        for part, (k_ref, v_ref) in enumerate(((ka_ref, va_ref), (kb_ref, vb_ref))):
            cols = slice((PARTS * j + part) * D, (PARTS * j + part + 1) * D)
            dk_ref[:, cols] = k_ref[j]
            dv_ref[:, cols] = v_ref[j]


def join(ka, kb, va, vb):
    vmem = pl.BlockSpec(memory_space=pltpu.VMEM)
    full = jax.ShapeDtypeStruct((TOK, KV_HEADS * D), jnp.bfloat16)
    return pl.pallas_call(
        join_kernel,
        in_specs=[vmem] * 4,
        out_specs=[vmem] * 2,
        out_shape=[full] * 2,
        compiler_params=params(),
        cost_estimate=cost(1 << 20, MIB),
        name="join",
    )(ka, kb, va, vb)


def query_post_kernel(me_ref, *refs):
    out_ref = refs[8]
    for delta in range(4):

        @pl.when(pl.program_id(0) == delta)
        def _():
            out_ref[:, : REP * D] = refs[delta][...]
            out_ref[:, REP * D :] = refs[4 + delta][...]


def query_post(quad, a, b):
    source = pl.BlockSpec((TOK, REP * D), lambda i, me: (0, 0))
    return pl.pallas_call(
        query_post_kernel,
        grid_spec=pltpu.PrefetchScalarGridSpec(
            num_scalar_prefetch=1,
            grid=(4,),
            in_specs=[source] * 8,
            out_specs=pl.BlockSpec((TOK, PARTS * REP * D), lambda i, me: (0, me[0] ^ i)),
        ),
        out_shape=jax.ShapeDtypeStruct((TOK, HEADS * D), jnp.bfloat16),
        compiler_params=params(),
        cost_estimate=cost(1 << 20, 4 * MIB),
        name="query_post",
    )(quad, *a, *b)


def project_kernel(*refs):
    nn = ((1,), (0,))
    total = dot(refs[0][...], refs[8][...], nn)
    for i in range(1, 8):
        total += dot(refs[i][...], refs[8 + i][...], nn)
    total = total.astype(jnp.bfloat16)
    if len(refs) == 17:
        refs[16][...] = total
    else:
        refs[17][:, : 2 * D] = refs[16][...]
        refs[17][:, 2 * D :] = total


def project(xt, kg, earlier=()):
    width = 2 * D * (1 + len(earlier))
    return pl.pallas_call(
        project_kernel,
        grid=(2,),
        in_specs=[pl.BlockSpec((512, TOK), lambda i: (i, 0))] * 8
        + [pl.BlockSpec((TOK, 2 * D), lambda i: (0, 0))] * 8
        + [pl.BlockSpec((512, 2 * D), lambda i: (i, 0))] * len(earlier),
        out_specs=pl.BlockSpec((512, width), lambda i: (i, 0)),
        out_shape=jax.ShapeDtypeStruct((1024, width), jnp.bfloat16),
        compiler_params=params(),
        cost_estimate=cost(10**9, 3 * MIB),
        name="project",
    )(*xt, *kg, *earlier)


def final_sum_kernel(in_ref, out_ref):
    for c in range(2):
        total = jnp.zeros((16, PARTS * 2 * D), jnp.float32)
        for s in range(16):
            for zh in range(2):
                total += in_ref[s, c, zh].astype(jnp.float32)
        for part in range(PARTS):
            for side in range(2):
                head = (2 * c + side) * PARTS + part
                at = (part * 2 + side) * D
                out_ref[:, head * D : (head + 1) * D] = total[:, at : at + D]


def final_sum(pieces):
    vmem = pl.BlockSpec(memory_space=pltpu.VMEM)
    return pl.pallas_call(
        final_sum_kernel,
        in_specs=[vmem],
        out_specs=vmem,
        out_shape=jax.ShapeDtypeStruct((16, 1024), jnp.float32),
        compiler_params=params(),
        cost_estimate=cost(1 << 20, MIB),
        name="final_sum",
    )(pieces.reshape(16, 2, 2, 16, PARTS * 2 * D))


def local(q, k, v, g, x, group_first, seq_length, pos_offset):
    me = lax.axis_index("sp")
    first, length, offset = group_first[0], seq_length[0], pos_offset[0]
    rates = jnp.exp(jnp.arange(HALF, dtype=jnp.float32) * (-2.0 * math.log(10000.0) / D))
    token = jnp.arange(TOK, dtype=jnp.int32)

    own = (me - first[me]) * TOK + token
    phase = (offset[me] + own).astype(jnp.float32)[:, None] * rates[None, :]
    cos, sin = jnp.cos(phase), jnp.sin(phase)
    cos = jnp.concatenate([cos, cos], -1)
    sin = jnp.concatenate([-sin, sin], -1)
    valid = jnp.broadcast_to((own < length[me]).astype(jnp.float32)[:, None], (TOK, D))

    half = me // 16
    z = me % 8 // 2
    core = me % 2
    quad = me // 8 % 2 * 2 + core
    y = lax.axis_index("dp") // 2
    beside = (me // 8 % 2) ^ jnp.arange(2, dtype=jnp.int32)
    device = half * 16 + beside * 8 + z * 2
    start = first[device]
    before = (device - start) * TOK
    meta = jnp.stack(
        [
            (start - half * 16) // 2,
            (device - half * 16) // 2,
            jnp.clip(length[device] - before, 0, CHUNK),
            jnp.broadcast_to(core, (2,)),
        ],
        axis=1,
    )
    inside = jnp.arange(CHUNK, dtype=jnp.int32) ^ (core * TOK)
    place = (offset[device] + before)[:, None] + inside[None, :]
    turned = place.astype(jnp.float32)[:, None, :] * rates[None, :, None]
    cos_t, sin_t = jnp.cos(turned), jnp.sin(turned)
    row = half * 16 + jnp.arange(16, dtype=jnp.int32)
    row_start = offset[row] + (row - first[row]) * TOK
    row_place = (row_start[:, None] + token[None, :]).reshape(CHUNKS, CHUNK)
    row_phase = row_place.astype(jnp.float32)[:, :, None] * rates[None, None, :]
    row_cos, row_sin = jnp.cos(row_phase), jnp.sin(row_phase)
    row_cos = jnp.concatenate([row_cos, row_cos], -1)
    row_sin = jnp.concatenate([-row_sin, row_sin], -1)
    quad_at, y_at, core_at = (i.astype(jnp.int32).reshape(1) for i in (quad, y, core))

    def quad_swap(pieces):
        return [pieces[0]] + [quad_send(pieces[d], d) for d in range(1, 4)]

    def query_pieces(part, deltas):
        return query_prep(part, deltas, quad_at, q[0], g[0], cos, sin, valid)

    def quad_swap(pieces):
        return [quad_send(piece, d + 1) for d, piece in enumerate(pieces)]

    sent = query_pieces(0, (1, 2, 3))
    qg_in = [quad_swap(sent)]
    kv_out = [a.reshape(16, 2, TOK, D) for a in key_send(k[0], v[0])]
    kv_in = [swap(kv_out[0], "sp", HALF_GROUPS)]
    xt = [a.reshape(1024, TOK) for a in input_prep(y_at, after(x[0], qg_in[0][0]))]
    xt = [xt[0]] + [y_send(xt[step], step) for step in range(1, 4)]
    qg_in[0] = list(query_pieces(0, (0,))) + qg_in[0]
    kv_in[0] = after(kv_in[0], *xt)

    own = query_pieces(1, (0,))
    sent = query_pieces(1, (1, 2, 3))
    qg_in.append(list(own) + quad_swap([after(piece, *qg_in[0]) for piece in sent]))
    kv_in.append(swap(after(kv_out[1], kv_in[0]), "sp", HALF_GROUPS))
    xt = xt + [y_send(a, 0, 1) for a in xt]
    kv_in[1] = after(kv_in[1], *xt)

    dq_back, dkv_back = [], []
    for part in range(PARTS):
        keys = key_turn(kv_in[part], row_cos, row_sin)
        *dq, dkv = attention(meta, qg_in[part], keys, cos_t, sin_t)
        for earlier in dq_back:
            dkv = after(dkv, *earlier)
        dkv_back.append(swap(dkv, "sp", HALF_GROUPS))
        dq_back.append([dq[0]] + quad_swap(dq[1:]))

    dk, dv, partial = [], [], ()
    for part in range(PARTS):
        back = after(dkv_back[part], *dq_back[part], *partial)
        dk_part, dv_part, same, other = key_post(core_at, back, cos, sin)
        dk.append(dk_part)
        dv.append(dv_part)
        kg = [same] + [y_send(same, step) for step in range(1, 4)]
        kg += [y_send(other, step, 1) for step in range(4)]
        partial = (project(xt, kg, partial),)
    pieces = swap(partial[0].reshape(64, 16, 4 * D), ("sp", "dp"), PLANE_GROUPS)
    kproj_grad = final_sum(pieces)
    key_gradient, value_gradient = join(*dk, *dv)
    query_grad = query_post(quad_at, *dq_back)
    return (query_grad[None], key_gradient[None], value_gradient[None], kproj_grad)


def solution(mesh):
    tokens = P("dp", "sp", None)
    table = P("dp", None)
    return jax.shard_map(
        local,
        mesh=mesh,
        in_specs=(tokens,) * 5 + (table,) * 3,
        out_specs=(tokens, tokens, tokens, P(("sp", "dp"), None)),
        check_vma=False,
    )
```

```python
import math

import jax
import jax.numpy as jnp
from jax import lax
from jax.experimental import pallas as pl
from jax.experimental.pallas import tpu as pltpu
from jax.sharding import PartitionSpec as P

HEADS = 64
KV_HEADS = 8
D = 128
HALF = D // 2
TOK = 128
SP = 32
PARTS = 2
REP = HEADS // KV_HEADS
CHUNK = 2 * TOK
CHUNKS = 8
STACK = 4
ROWS = STACK * CHUNK
SCALE = D ** (-0.5)
LOG2E = 1.4426950408889634
MIB = 1 << 20

HALF_GROUPS = [list(range(16)), list(range(16, 32))]
PLANE_GROUPS = [
    [s * 8 + y * 2 + zh for s in range(SP) for zh in range(2)] for y in range(4)
]


def swap(array, axes, groups):
    return lax.all_to_all(
        array, axes, split_axis=0, concat_axis=0, axis_index_groups=groups, tiled=True
    )


def quad_send(array, delta):
    flip = (delta & 1) | (delta >> 1) << 3
    return lax.ppermute(array, "sp", [(s, s ^ flip) for s in range(SP)])


def y_send(array, step, core=0):
    pairs = []
    for s in range(SP):
        for d in range(8):
            to = ((d // 2 + step) % 4) * 2 + d % 2
            pairs.append((s * 8 + d, (s ^ core) * 8 + to))
    return lax.ppermute(array, ("sp", "dp"), pairs)


def after(array, *earlier):
    return lax.optimization_barrier((array, *earlier))[0]


def params(limit=12):
    return pltpu.CompilerParams(vmem_limit_bytes=limit * MIB)


def cost(flops, nbytes):
    return pl.CostEstimate(flops=flops, bytes_accessed=nbytes, transcendentals=0)


def dot(a, b, dims):
    return lax.dot_general(a, b, (dims, ((), ())), preferred_element_type=jnp.float32)


def turn(x, cos, sin):
    return x * cos + pltpu.roll(x, HALF, 1) * sin


def key_prep_kernel(k_ref, v_ref, cos_ref, sin_ref, *outs):
    cos, sin = cos_ref[...], sin_ref[...]
    for part in range(PARTS):
        cols = slice(part * D, (part + 1) * D)
        k = turn(k_ref[:, cols].astype(jnp.float32), cos, sin).astype(jnp.bfloat16)
        v = v_ref[:, cols]
        for z in range(4):
            outs[part][0, z, 0, 0] = k
            outs[part][0, z, 0, 1] = v


def key_prep(k, v, cos, sin):
    table = pl.BlockSpec((TOK, D), lambda j: (0, 0))
    column = pl.BlockSpec((TOK, PARTS * D), lambda j: (0, j))
    shape = jax.ShapeDtypeStruct((2, 4, 2, 2, TOK, D), jnp.bfloat16)
    return pl.pallas_call(
        key_prep_kernel,
        grid=(4,),
        in_specs=[column, column, table, table],
        out_specs=[
            pl.BlockSpec((1, 4, 1, 2, TOK, D), lambda j: (j // 2, 0, j % 2, 0, 0, 0))
        ]
        * PARTS,
        out_shape=[shape] * PARTS,
        compiler_params=params(),
        cost_estimate=cost(1 << 20, 3 * MIB),
        name="key_prep",
    )(k, v, cos, sin)


def query_prep_kernel(me_ref, q_ref, g_ref, cos_ref, sin_ref, valid_ref, *outs):
    cos, sin = cos_ref[...], sin_ref[...]
    keep = valid_ref[...] > 0.0
    for at, out in enumerate(outs):

        @pl.when(pl.program_id(0) == at)
        def _():
            for h in range(REP):
                cols = slice(h * D, (h + 1) * D)
                q = turn(q_ref[:, cols].astype(jnp.float32), cos, sin)
                out[0, :, cols] = q.astype(jnp.bfloat16)
                g = jnp.where(keep, g_ref[:, cols].astype(jnp.float32), 0.0)
                out[1, :, cols] = g.astype(jnp.bfloat16)


def query_prep(part, deltas, quad, q, g, cos, sin, valid):
    count, low = len(deltas), deltas[0]
    first = part == 0 and low == 1
    table = pl.BlockSpec((TOK, D), lambda i, me: (0, 0))
    column = pl.BlockSpec(
        (TOK, REP * D), lambda i, me: (0, (me[0] ^ (i + low)) * PARTS + part)
    )
    shape = jax.ShapeDtypeStruct((2, TOK, REP * D), jnp.bfloat16)
    return pl.pallas_call(
        query_prep_kernel,
        grid_spec=pltpu.PrefetchScalarGridSpec(
            num_scalar_prefetch=1,
            grid=(count,),
            in_specs=[column, column, table, table, table],
            out_specs=[pl.BlockSpec((2, TOK, REP * D), lambda i, me: (0, 0, 0))] * count,
        ),
        out_shape=[shape] * count,
        compiler_params=params(56 if first else 12),
        cost_estimate=cost(count << 20, count * MIB),
        name="query_prep",
    )(quad, q, g, cos, sin, valid)


def input_prep_kernel(me_ref, x_ref, *refs):
    outs, flipped = refs[:4], refs[4]
    for s in range(4):
        flipped[...] = x_ref[:, s * TOK : (s + 1) * TOK].T
        for step in range(4):
            at = pl.multiple_of((me_ref[0] + step) % 4 * 32, 32)
            outs[step][s] = flipped[pl.ds(at, 32)]


def input_prep(y, x):
    return pl.pallas_call(
        input_prep_kernel,
        grid_spec=pltpu.PrefetchScalarGridSpec(
            num_scalar_prefetch=1,
            grid=(8,),
            in_specs=[pl.BlockSpec((TOK, 512), lambda i, me: (0, i))],
            out_specs=[pl.BlockSpec((4, 32, TOK), lambda i, me: (i, 0, 0))] * 4,
            scratch_shapes=[pltpu.VMEM((TOK, TOK), jnp.bfloat16)],
        ),
        out_shape=[jax.ShapeDtypeStruct((SP, 32, TOK), jnp.bfloat16)] * 4,
        compiler_params=params(),
        cost_estimate=cost(1 << 20, 2 * MIB),
        name="input_prep",
    )(y, x)


def attention_kernel(meta_ref, *refs):
    qg_refs, (kv_ref, cos_ref, sin_ref) = refs[:4], refs[4:7]
    dq_refs, dkv_ref = refs[7:11], refs[11]
    kt_ref, e_ref, dp_ref, peak_ref, dk_ref, dv_ref, dqt_ref = refs[12:]
    heads = pl.program_id(0)
    nt, nn = ((1,), (1,)), ((1,), (0,))

    def keys(p, which):
        return kv_ref[pl.ds(2 * p, 2), which].reshape(CHUNK, D)

    @pl.when(heads == 0)
    def _():
        dk_ref[...] = jnp.zeros_like(dk_ref)
        dv_ref[...] = jnp.zeros_like(dv_ref)
        for p in range(CHUNKS):
            kt_ref[p] = keys(p, 0).T

    def attend(block):
        low, diagonal = meta_ref[block, 0], meta_ref[block, 1]
        count, core = meta_ref[block, 2], meta_ref[block, 3]

        def stacked(which):
            return jnp.concatenate(
                [
                    qg_refs[2 * block + other][which, :, h * D : (h + 1) * D]
                    for h in range(STACK)
                    for other in range(2)
                ],
                axis=0,
            )

        @pl.when(count <= 0)
        def _():
            for other in range(2):
                ref = dq_refs[2 * block + other]
                ref[...] = jnp.zeros_like(ref)

        @pl.when(count > 0)
        def _():
            q, g = stacked(0), stacked(1)

            def score(p, state, allowed=None):
                peak, total, mixed = state
                s = dot(keys(p, 0), q, nt)
                if allowed is not None:
                    s = jnp.where(allowed, s, -1e30)
                dp = dot(keys(p, 1), g, nt)
                dp_ref[p] = dp
                higher = jnp.maximum(peak, jnp.max(s, axis=0, keepdims=True))
                shrink = jnp.exp2((peak - higher) * (SCALE * LOG2E))
                e = jnp.exp2((s - higher) * (SCALE * LOG2E))
                e_ref[p] = e
                peak_ref[p] = higher
                return (
                    higher,
                    total * shrink + jnp.sum(e, axis=0, keepdims=True),
                    mixed * shrink + jnp.sum(e * dp, axis=0, keepdims=True),
                )

            zero = jnp.zeros((1, ROWS), jnp.float32)
            state = (jnp.full((1, ROWS), -1e30, jnp.float32), zero, zero)
            state = lax.fori_loop(low, diagonal, score, state)
            key_at = lax.broadcasted_iota(jnp.int32, (CHUNK, ROWS), 0)
            row_at = lax.broadcasted_iota(jnp.int32, (CHUNK, ROWS), 1) & (CHUNK - 1)
            row_at = row_at ^ (core * TOK)
            allowed = (key_at <= row_at) & (key_at < count)
            peak, total, mixed = score(diagonal, state, allowed)
            inverse = 1.0 / total
            row_dot = mixed * inverse
            dqt_ref[...] = jnp.zeros_like(dqt_ref)

            def spread(p, carry):
                factor = jnp.exp2((peak_ref[p] - peak) * (SCALE * LOG2E)) * inverse
                weights = e_ref[p] * factor
                ds = (weights * (dp_ref[p] - row_dot)).astype(jnp.bfloat16)
                dv_ref[p] += dot(weights.astype(jnp.bfloat16), g, nn)
                dk_ref[p] += dot(ds, q, nn)
                dqt_ref[...] += dot(kt_ref[p], ds, nn)
                return carry

            lax.fori_loop(low, diagonal + 1, spread, 0)
            cos, sin = cos_ref[block], sin_ref[block]
            for h in range(STACK):
                cols = slice(h * CHUNK, (h + 1) * CHUNK)
                x1 = dqt_ref[:HALF, cols] * SCALE
                x2 = dqt_ref[HALF:, cols] * SCALE
                y = jnp.concatenate([x1 * cos + x2 * sin, x2 * cos - x1 * sin], axis=0)
                y = y.T.astype(jnp.bfloat16)
                for other in range(2):
                    dq_refs[2 * block + other][:, h * D : (h + 1) * D] = y[
                        other * TOK : (other + 1) * TOK
                    ]

    attend(0)
    attend(1)

    @pl.when(heads == REP // STACK - 1)
    def _():
        for p in range(CHUNKS):
            dk = (dk_ref[p] * SCALE).astype(jnp.bfloat16)
            dkv_ref[2 * p : 2 * p + 2, 0] = dk.reshape(2, TOK, D)
            dkv_ref[2 * p : 2 * p + 2, 1] = dv_ref[p].astype(jnp.bfloat16).reshape(2, TOK, D)


def attention(meta, qg, kv, cos, sin):
    width = STACK * D
    table = pl.BlockSpec((2, HALF, CHUNK), lambda h: (0, 0, 0))
    whole = pl.BlockSpec((16, 2, TOK, D), lambda h: (0, 0, 0, 0))
    return pl.pallas_call(
        attention_kernel,
        grid=(REP // STACK,),
        in_specs=[pl.BlockSpec(memory_space=pltpu.SMEM)]
        + [pl.BlockSpec((2, TOK, width), lambda h: (0, 0, h))] * 4
        + [whole, table, table],
        out_specs=[pl.BlockSpec((TOK, width), lambda h: (0, h))] * 4 + [whole],
        out_shape=[jax.ShapeDtypeStruct((TOK, REP * D), jnp.bfloat16)] * 4
        + [jax.ShapeDtypeStruct((16, 2, TOK, D), jnp.bfloat16)],
        scratch_shapes=[
            pltpu.VMEM((CHUNKS, D, CHUNK), jnp.bfloat16),
            pltpu.VMEM((CHUNKS, CHUNK, ROWS), jnp.float32),
            pltpu.VMEM((CHUNKS, CHUNK, ROWS), jnp.float32),
            pltpu.VMEM((CHUNKS, 1, ROWS), jnp.float32),
            pltpu.VMEM((CHUNKS, CHUNK, D), jnp.float32),
            pltpu.VMEM((CHUNKS, CHUNK, D), jnp.float32),
            pltpu.VMEM((D, ROWS), jnp.float32),
        ],
        compiler_params=params(34),
        cost_estimate=cost(25 * 10**9, 6 * MIB),
        name="attention",
    )(meta, *qg, kv, cos, sin)


def key_post_kernel(core_ref, in_ref, cos_ref, sin_ref, dk_ref, dv_ref, same_ref, other_ref):
    cos, sin = cos_ref[...], sin_ref[...]
    dk = in_ref[0, 0, 0, 0].astype(jnp.float32)
    dv = in_ref[0, 0, 0, 1].astype(jnp.float32)
    for z in range(1, 4):
        dk += in_ref[0, z, 0, 0].astype(jnp.float32)
        dv += in_ref[0, z, 0, 1].astype(jnp.float32)
    dk = turn(dk, cos, -sin).astype(jnp.bfloat16)
    dk_ref[0] = dk
    dv_ref[0] = dv.astype(jnp.bfloat16)
    quad = pl.program_id(0)
    for side in range(2):
        cols = slice(side * D, (side + 1) * D)

        @pl.when((quad % 2 == side) & (quad // 2 == core_ref[0]))
        def _():
            same_ref[:, cols] = dk

        @pl.when((quad % 2 == side) & (quad // 2 != core_ref[0]))
        def _():
            other_ref[:, cols] = dk


def key_post(core, back, cos, sin):
    table = pl.BlockSpec((TOK, D), lambda j, me: (0, 0))
    piece = pl.BlockSpec((TOK, 2 * D), lambda j, me: (0, 0))
    lane = pl.BlockSpec((1, TOK, D), lambda j, me: (j, 0, 0))
    full = jax.ShapeDtypeStruct((4, TOK, D), jnp.bfloat16)
    sent = jax.ShapeDtypeStruct((TOK, 2 * D), jnp.bfloat16)
    return pl.pallas_call(
        key_post_kernel,
        grid_spec=pltpu.PrefetchScalarGridSpec(
            num_scalar_prefetch=1,
            grid=(4,),
            in_specs=[
                pl.BlockSpec(
                    (1, 4, 1, 2, TOK, D), lambda j, me: (j // 2, 0, j % 2, 0, 0, 0)
                ),
                table,
                table,
            ],
            out_specs=[lane, lane, piece, piece],
        ),
        out_shape=[full, full, sent, sent],
        compiler_params=params(),
        cost_estimate=cost(1 << 20, 2 * MIB),
        name="key_post",
    )(core, back.reshape(2, 4, 2, 2, TOK, D), cos, sin)


def join_kernel(ka_ref, kb_ref, va_ref, vb_ref, dk_ref, dv_ref):
    for j in range(4):
        for part, (k_ref, v_ref) in enumerate(((ka_ref, va_ref), (kb_ref, vb_ref))):
            cols = slice((PARTS * j + part) * D, (PARTS * j + part + 1) * D)
            dk_ref[:, cols] = k_ref[j]
            dv_ref[:, cols] = v_ref[j]


def join(ka, kb, va, vb):
    vmem = pl.BlockSpec(memory_space=pltpu.VMEM)
    full = jax.ShapeDtypeStruct((TOK, KV_HEADS * D), jnp.bfloat16)
    return pl.pallas_call(
        join_kernel,
        in_specs=[vmem] * 4,
        out_specs=[vmem] * 2,
        out_shape=[full] * 2,
        compiler_params=params(),
        cost_estimate=cost(1 << 20, MIB),
        name="join",
    )(ka, kb, va, vb)


def query_post_kernel(me_ref, *refs):
    out_ref = refs[8]
    for delta in range(4):

        @pl.when(pl.program_id(0) == delta)
        def _():
            out_ref[:, : REP * D] = refs[delta][...]
            out_ref[:, REP * D :] = refs[4 + delta][...]


def query_post(quad, a, b):
    source = pl.BlockSpec((TOK, REP * D), lambda i, me: (0, 0))
    return pl.pallas_call(
        query_post_kernel,
        grid_spec=pltpu.PrefetchScalarGridSpec(
            num_scalar_prefetch=1,
            grid=(4,),
            in_specs=[source] * 8,
            out_specs=pl.BlockSpec((TOK, PARTS * REP * D), lambda i, me: (0, me[0] ^ i)),
        ),
        out_shape=jax.ShapeDtypeStruct((TOK, HEADS * D), jnp.bfloat16),
        compiler_params=params(),
        cost_estimate=cost(1 << 20, 4 * MIB),
        name="query_post",
    )(quad, *a, *b)


def project_kernel(*refs):
    nn = ((1,), (0,))
    total = dot(refs[0][...], refs[8][...], nn)
    for i in range(1, 8):
        total += dot(refs[i][...], refs[8 + i][...], nn)
    total = total.astype(jnp.bfloat16)
    if len(refs) == 17:
        refs[16][...] = total
    else:
        refs[17][:, : 2 * D] = refs[16][...]
        refs[17][:, 2 * D :] = total


def project(xt, kg, earlier=()):
    width = 2 * D * (1 + len(earlier))
    return pl.pallas_call(
        project_kernel,
        grid=(2,),
        in_specs=[pl.BlockSpec((512, TOK), lambda i: (i, 0))] * 8
        + [pl.BlockSpec((TOK, 2 * D), lambda i: (0, 0))] * 8
        + [pl.BlockSpec((512, 2 * D), lambda i: (i, 0))] * len(earlier),
        out_specs=pl.BlockSpec((512, width), lambda i: (i, 0)),
        out_shape=jax.ShapeDtypeStruct((1024, width), jnp.bfloat16),
        compiler_params=params(),
        cost_estimate=cost(10**9, 3 * MIB),
        name="project",
    )(*xt, *kg, *earlier)


def final_sum_kernel(in_ref, out_ref):
    for c in range(2):
        total = jnp.zeros((16, PARTS * 2 * D), jnp.float32)
        for s in range(16):
            for zh in range(2):
                total += in_ref[s, c, zh].astype(jnp.float32)
        for part in range(PARTS):
            for side in range(2):
                head = (2 * c + side) * PARTS + part
                at = (part * 2 + side) * D
                out_ref[:, head * D : (head + 1) * D] = total[:, at : at + D]


def final_sum(pieces):
    vmem = pl.BlockSpec(memory_space=pltpu.VMEM)
    return pl.pallas_call(
        final_sum_kernel,
        in_specs=[vmem],
        out_specs=vmem,
        out_shape=jax.ShapeDtypeStruct((16, 1024), jnp.float32),
        compiler_params=params(),
        cost_estimate=cost(1 << 20, MIB),
        name="final_sum",
    )(pieces.reshape(16, 2, 2, 16, PARTS * 2 * D))


def local(q, k, v, g, x, group_first, seq_length, pos_offset):
    me = lax.axis_index("sp")
    first, length, offset = group_first[0], seq_length[0], pos_offset[0]
    rates = jnp.exp(jnp.arange(HALF, dtype=jnp.float32) * (-2.0 * math.log(10000.0) / D))
    token = jnp.arange(TOK, dtype=jnp.int32)

    own = (me - first[me]) * TOK + token
    phase = (offset[me] + own).astype(jnp.float32)[:, None] * rates[None, :]
    cos, sin = jnp.cos(phase), jnp.sin(phase)
    cos = jnp.concatenate([cos, cos], -1)
    sin = jnp.concatenate([-sin, sin], -1)
    valid = jnp.broadcast_to((own < length[me]).astype(jnp.float32)[:, None], (TOK, D))

    half = me // 16
    z = me % 8 // 2
    core = me % 2
    quad = me // 8 % 2 * 2 + core
    y = lax.axis_index("dp") // 2
    beside = (me // 8 % 2) ^ jnp.arange(2, dtype=jnp.int32)
    device = half * 16 + beside * 8 + z * 2
    start = first[device]
    before = (device - start) * TOK
    meta = jnp.stack(
        [
            (start - half * 16) // 2,
            (device - half * 16) // 2,
            jnp.clip(length[device] - before, 0, CHUNK),
            jnp.broadcast_to(core, (2,)),
        ],
        axis=1,
    )
    inside = jnp.arange(CHUNK, dtype=jnp.int32) ^ (core * TOK)
    place = (offset[device] + before)[:, None] + inside[None, :]
    turned = place.astype(jnp.float32)[:, None, :] * rates[None, :, None]
    cos_t, sin_t = jnp.cos(turned), jnp.sin(turned)
    quad_at, y_at, core_at = (i.astype(jnp.int32).reshape(1) for i in (quad, y, core))

    def quad_swap(pieces):
        return [pieces[0]] + [quad_send(pieces[d], d) for d in range(1, 4)]

    def query_pieces(part, deltas):
        return query_prep(part, deltas, quad_at, q[0], g[0], cos, sin, valid)

    def quad_swap(pieces):
        return [quad_send(piece, d + 1) for d, piece in enumerate(pieces)]

    sent = query_pieces(0, (1, 2, 3))
    qg_in = [quad_swap(sent)]
    kv_out = key_prep(after(k[0], *sent), v[0], cos, sin)
    kv_out = [a.reshape(16, 2, TOK, D) for a in kv_out]
    kv_in = [swap(kv_out[0], "sp", HALF_GROUPS)]
    xt = [a.reshape(1024, TOK) for a in input_prep(y_at, after(x[0], qg_in[0][0]))]
    xt = [xt[0]] + [y_send(xt[step], step) for step in range(1, 4)]
    qg_in[0] = list(query_pieces(0, (0,))) + qg_in[0]
    kv_in[0] = after(kv_in[0], *xt)

    own = query_pieces(1, (0,))
    sent = query_pieces(1, (1, 2, 3))
    qg_in.append(list(own) + quad_swap([after(piece, *qg_in[0]) for piece in sent]))
    kv_in.append(swap(after(kv_out[1], kv_in[0]), "sp", HALF_GROUPS))
    xt = xt + [y_send(a, 0, 1) for a in xt]
    kv_in[1] = after(kv_in[1], *xt)

    dq_back, dkv_back = [], []
    for part in range(PARTS):
        *dq, dkv = attention(meta, qg_in[part], kv_in[part], cos_t, sin_t)
        for earlier in dq_back:
            dkv = after(dkv, *earlier)
        dkv_back.append(swap(dkv, "sp", HALF_GROUPS))
        dq_back.append([dq[0]] + quad_swap(dq[1:]))

    dk, dv, partial = [], [], ()
    for part in range(PARTS):
        back = after(dkv_back[part], *dq_back[part], *partial)
        dk_part, dv_part, same, other = key_post(core_at, back, cos, sin)
        dk.append(dk_part)
        dv.append(dv_part)
        kg = [same] + [y_send(same, step) for step in range(1, 4)]
        kg += [y_send(other, step, 1) for step in range(4)]
        partial = (project(xt, kg, partial),)
    pieces = swap(partial[0].reshape(64, 16, 4 * D), ("sp", "dp"), PLANE_GROUPS)
    kproj_grad = final_sum(pieces)
    key_gradient, value_gradient = join(*dk, *dv)
    query_grad = query_post(quad_at, *dq_back)
    return (query_grad[None], key_gradient[None], value_gradient[None], kproj_grad)


def solution(mesh):
    tokens = P("dp", "sp", None)
    table = P("dp", None)
    return jax.shard_map(
        local,
        mesh=mesh,
        in_specs=(tokens,) * 5 + (table,) * 3,
        out_specs=(tokens, tokens, tokens, P(("sp", "dp"), None)),
        check_vma=False,
    )
```
